512 devices in a mesh: tm: 32 (over y, x, core), stream: 16 (over z).
Axes of the slice: x: 4, y: 4, z: 16, core: 2. Of those that a mesh axis runs over, the one named last changes fastest.
Arguments:
- tokens: bfloat16 [65536, 2048], P(('tm', 'stream')), may hold values from -6 to 6
- w_query: bfloat16 [2048, 2048], P('stream'), may hold values from -0.125 to 0.125
- w_key: bfloat16 [2048, 2048], P('stream'), may hold values from -0.125 to 0.125
- w_value: bfloat16 [2048, 2048], P('stream'), may hold values from -0.125 to 0.125
- decay_proj: bfloat16 [2048, 16], P('stream'), may hold values from -0.125 to 0.125
- beta_proj: bfloat16 [2048, 16], P('stream'), may hold values from -0.125 to 0.125
- decay_rate: float32 [16], replicated, may hold values from 1.5258789e-05 to 0.1
- beta_bias: float32 [16], replicated, may hold values from -7 to 0
- norm_gain: float32 [128], replicated, may hold values from 0.5 to 1.5
Outputs:
- mixed: bfloat16 [65536, 2048], P(('tm', 'stream'))
The draws below stay inside these ranges and needn't reach their ends.
All inputs are finite; a program needn't handle non-finite values.
Results may differ from the reference program's by a relative error of at most 0.0073.
Values may be sent and summed in bfloat16 or wider, within the bound.
No kernel may reach another device: no remote copies, remote signals or barrier semaphores. Data moves between devices by JAX's collectives and lax.ppermute only.
A program may use at most 128 MiB of HBM per device.

```python
import math
import jax
import jax.numpy as jnp
from jax import lax

D = 2048
HEADS = 16
DK = 128
DV = 128
GROUP = 256
TOKENS = 65536


def steps_of(rng, dims, split, smallest, largest):
    def one(axis_at, parts):
        heights = jax.random.uniform(jax.random.fold_in(jax.random.fold_in(rng, 6), axis_at), (parts,), jnp.float32, smallest / len(split), largest / len(split))
        return jnp.repeat(jnp.exp(heights), dims[axis_at] // parts).reshape((-1,) + (1,) * (len(dims) - axis_at - 1))

    loudness = one(*split[0])
    for cut in split[1:]:
        loudness = loudness * one(*cut)
    return loudness


def centred(own_key, dims, deviation, limit, cuts=(), held_as=jnp.bfloat16):
    entries = jax.random.normal(own_key, dims, jnp.float32) * deviation
    if len(cuts) > 0:
        entries = steps_of(own_key, dims, cuts, -0.22, 0.18) * entries
    return jnp.clip(entries, min=-limit, max=limit).astype(held_as)


def setup_inputs(seed: int = 0) -> dict:
    key_list = jax.random.split(jax.random.key(seed), 10)
    tokens = centred(key_list[0], (TOKENS, D), 1.0, 6.0, ((0, 512),))
    w_query = centred(key_list[1], (D, HEADS * DK), D ** -0.5, 0.125, ((0, 16),))
    w_key = centred(key_list[2], (D, HEADS * DK), D ** -0.5, 0.125, ((0, 16),))
    w_value = centred(key_list[3], (D, HEADS * DV), D ** -0.5, 0.125, ((0, 16),))
    decay_proj = centred(key_list[4], (D, HEADS), D ** -0.5, 0.125, ((0, 16),))
    beta_proj = centred(key_list[5], (D, HEADS), D ** -0.5, 0.125, ((0, 16),))
    decay_rate = jnp.clip(jnp.exp(jax.random.uniform(key_list[6], (HEADS,), jnp.float32, math.log(1.52587890625e-05), math.log(0.1))), 1.52587890625e-05, 0.1)
    beta_bias = jnp.clip(jax.random.uniform(key_list[7], (HEADS,), jnp.float32, -7.0, 0.0), -7.0, 0.0)
    norm_gain = jnp.clip(1.0 + 0.1 * jax.random.normal(key_list[8], (DV,), jnp.float32), 0.5, 1.5)
    return {"tokens": tokens, "w_query": w_query, "w_key": w_key, "w_value": w_value, "decay_proj": decay_proj, "beta_proj": beta_proj, "decay_rate": decay_rate, "beta_bias": beta_bias, "norm_gain": norm_gain}


highest_precision = lax.Precision.HIGHEST

def narrowed(value):
    return lax.optimization_barrier(value.astype(jnp.bfloat16)).astype(jnp.float32)

def reference(tokens, w_query, w_key, w_value, decay_proj, beta_proj, decay_rate, beta_bias, norm_gain):
    num_blocks = TOKENS // GROUP
    query_mat = w_query.astype(jnp.float32)
    key_mat = w_key.astype(jnp.float32)
    value_mat = w_value.astype(jnp.float32)
    decay_mat_w = decay_proj.astype(jnp.float32)
    beta_mat_w = beta_proj.astype(jnp.float32)
    blocks = tokens.reshape(num_blocks, GROUP, D)
    positions = jnp.arange(GROUP)
    strict = positions[:, None] > positions[None, :]
    inclusive_mask = positions[:, None] >= positions[None, :]
    identity = jnp.eye(GROUP, dtype=jnp.float32)

    def advance(state, block_rows):
        inputs = block_rows.astype(jnp.float32)
        raw_query = jnp.dot(inputs, query_mat, precision=highest_precision).reshape(GROUP, HEADS, DK)
        raw_key = jnp.dot(inputs, key_mat, precision=highest_precision).reshape(GROUP, HEADS, DK)
        queries = narrowed(raw_query * lax.rsqrt(lax.optimization_barrier(jnp.sum(raw_query * raw_query, -1, keepdims=True)) + 1e-06) * DK ** (-0.5))
        key_rows = narrowed(raw_key * lax.rsqrt(lax.optimization_barrier(jnp.sum(raw_key * raw_key, -1, keepdims=True)) + 1e-06))
        values = narrowed(jnp.dot(inputs, value_mat, precision=highest_precision)).reshape(GROUP, HEADS, DV)
        log_decay = narrowed(-decay_rate * jax.nn.softplus(jnp.dot(inputs, decay_mat_w, precision=highest_precision)))
        strength = narrowed(jax.nn.sigmoid(jnp.dot(inputs, beta_mat_w, precision=highest_precision) + beta_bias))
        cumulative = jnp.cumsum(log_decay, axis=0).T
        growth = jnp.exp(cumulative)
        last_log = cumulative[:, -1:]
        tail = jnp.exp(last_log - cumulative)
        strength_t = strength.T
        query_per_head = queries.transpose(1, 0, 2)
        key_per_head = key_rows.transpose(1, 0, 2)
        value_h = values.transpose(1, 0, 2)
        key_products = jnp.einsum('rxz,rfz->rxf', key_per_head, key_per_head, precision=highest_precision)
        spread = cumulative[:, :, None] - cumulative[:, None, :]
        decay_matrix = jnp.exp(jnp.where(inclusive_mask, spread, 0.0))
        lower = jnp.where(strict, strength_t[:, :, None] * decay_matrix * key_products, 0.0) + identity
        right_side = jnp.concatenate([(strength_t * growth)[..., None] * key_per_head, strength_t[..., None] * value_h], -1)
        solved = jax.scipy.linalg.solve_triangular(lower, right_side, lower=True, unit_diagonal=True)
        weights_w = solved[..., :DK]
        updates = solved[..., DK:]
        key_tail = tail[..., None] * key_per_head
        attention_scores = jnp.where(inclusive_mask, jnp.einsum('rxz,rfz->rxf', query_per_head, key_per_head, precision=highest_precision) * decay_matrix, 0.0)
        query_grown = growth[..., None] * query_per_head
        fresh = updates - jnp.einsum('hcd,hed->hce', weights_w, state, precision=highest_precision)
        read = jnp.einsum('hcd,hed->hce', query_grown, state, precision=highest_precision) + jnp.einsum('hcm,hme->hce', attention_scores, fresh, precision=highest_precision)
        new_state = jnp.exp(last_log)[..., None] * state + jnp.einsum('hce,hcd->hed', fresh, key_tail, precision=highest_precision)
        readout = narrowed(read).transpose(1, 0, 2)
        normed = readout * lax.rsqrt(lax.optimization_barrier(jnp.mean(readout * readout, -1, keepdims=True)) + 1e-06) * norm_gain
        return (new_state, normed.reshape(GROUP, HEADS * DV).astype(jnp.bfloat16))
    start = jnp.zeros((HEADS, DV, DK), jnp.float32)
    final_state, outputs = lax.scan(advance, start, blocks)
    return outputs.reshape(TOKENS, HEADS * DV)
```

```python
import jax
import jax.numpy as jnp
from jax import lax
from jax.experimental import pallas as pl
from jax.experimental.pallas import tpu as pltpu
from jax.sharding import Mesh
from jax.sharding import PartitionSpec as P

HEADS = 16
DK = 128
DV = 128
CHUNK = 128
GANG = 8
WIDE = 512
TM_STREAM = ("tm_0", "tm_1", "tm_2", "stream")
f32 = jnp.float32
bf16 = jnp.bfloat16


def mm(a, b, ca=1, cb=0):
    return lax.dot_general(
        a.astype(bf16), b.astype(bf16), (((ca,), (cb,)), ((), ())), preferred_element_type=f32
    )


def mm_exact(a, b, ca=1, cb=0):
    return lax.dot_general(
        a, b, (((ca,), (cb,)), ((), ())), precision=lax.Precision.HIGHEST, preferred_element_type=f32
    )


def chunk_kernel(gate_ref, raw_ref, reach_ref, own_ref, total_ref):
    rate, bias = gate_ref[0], gate_ref[1]
    row = lax.broadcasted_iota(jnp.int32, (CHUNK, CHUNK), 0)
    col = lax.broadcasted_iota(jnp.int32, (CHUNK, CHUNK), 1)
    strict, inclusive = row > col, row >= col
    eye = jnp.where(row == col, 1.0, 0.0).astype(f32)
    ones_below = jnp.where(inclusive, 1.0, 0.0).astype(bf16)
    total_ref[0:DK, :] = eye
    total_ref[DK:, :] = jnp.zeros((DV, DK), f32)

    def below(size):
        return (
            (row // (2 * size) == col // (2 * size))
            & ((row // size) % 2 == 1)
            & ((col // size) % 2 == 0)
        )

    def gang(step, carry):
        starts = [pl.multiple_of((step * GANG + i) * CHUNK, CHUNK) for i in range(GANG)]
        each = range(GANG)
        q, k, v, beta, grow, scale_row, beta_row, tail, last, decay = ([] for _ in range(10))
        for i in each:
            raw_q = raw_ref[pl.ds(starts[i], CHUNK), 0:128]
            raw_k = raw_ref[pl.ds(starts[i], CHUNK), 128:256]
            raw_v = raw_ref[pl.ds(starts[i], CHUNK), 256:384]
            logits = raw_ref[pl.ds(starts[i], CHUNK), 384:512]
            q.append(
                (
                    raw_q
                    * lax.rsqrt(jnp.sum(raw_q * raw_q, -1, keepdims=True) + 1e-06)
                    * DK ** (-0.5)
                ).astype(bf16)
            )
            k.append(
                (raw_k * lax.rsqrt(jnp.sum(raw_k * raw_k, -1, keepdims=True) + 1e-06)).astype(bf16)
            )
            v.append(raw_v.astype(bf16))
            x = logits[:, 0:1]
            softplus = jnp.maximum(x, 0.0) + jnp.log1p(jnp.exp(-jnp.abs(x)))
            log_decay = (-rate * softplus).astype(bf16)
            strength = (1.0 / (1.0 + jnp.exp(-(logits[:, 1:2] + bias)))).astype(bf16).astype(f32)
            g = mm(ones_below, jnp.broadcast_to(log_decay, (CHUNK, CHUNK)))
            b = jnp.broadcast_to(strength, (CHUNK, CHUNK))
            turned = jnp.where(col < 64, g, b).T
            g_row, b_row = turned[0:1, :], turned[64:65, :]
            g_last = g_row[:, CHUNK - 1 : CHUNK]
            beta.append(b)
            grow.append(jnp.exp(g))
            beta_row.append(b_row)
            scale_row.append(b_row * jnp.exp(g_row))
            tail.append(jnp.exp(g_last - g))
            last.append(jnp.exp(g_last))
            decay.append(jnp.exp(jnp.where(inclusive, g - g_row, 0.0)))
        both = [mm(jnp.concatenate([q[i], k[i]], 0), k[i], 1, 1) for i in each]
        scores = [jnp.where(inclusive, both[i][:CHUNK] * decay[i], 0.0) for i in each]
        lower = [jnp.where(strict, beta[i] * decay[i] * both[i][CHUNK:], 0.0) for i in each]
        inverse = [eye - jnp.where(below(1), lower[i], 0.0) for i in each]
        for size in (2, 4, 8, 16, 32, 64):
            mask = below(size)
            inner = [mm(jnp.where(mask, lower[i], 0.0), inverse[i]) for i in each]
            inverse = [inverse[i] - mm(inverse[i], inner[i]) for i in each]
        rounded = [inverse[i].astype(bf16) for i in each]
        high = [lower[i].astype(bf16) for i in each]
        low = [(lower[i] - high[i].astype(f32)).astype(bf16) for i in each]
        rest = [
            eye - rounded[i].astype(f32) - mm(high[i], rounded[i]) - mm(low[i], rounded[i])
            for i in each
        ]
        inverse = [rounded[i].astype(f32) + mm(rounded[i], rest[i]) for i in each]
        w = [mm(inverse[i] * scale_row[i], k[i]) for i in each]
        u = [mm(inverse[i] * beta_row[i], v[i]) for i in each]
        wu = [jnp.concatenate([w[i], u[i]], 1) for i in each]
        tail2 = [jnp.concatenate([tail[i], tail[i]], 1) for i in each]
        change = [mm(wu[i] * tail2[i], k[i], 0, 0) for i in each]
        inside = [mm(scores[i], wu[i]) for i in each]
        reach = [grow[i] * q[i].astype(f32) - inside[i][:, :DK] for i in each]
        state = total_ref[...]
        for i in each:
            out = mm(reach[i], state, 1, 1)
            reach_ref[pl.ds(starts[i], CHUNK), :] = out[:, :DK].astype(bf16)
            own_ref[pl.ds(starts[i], CHUNK), :] = out[:, DK:] + inside[i][:, DK:]
            moved = mm(state, change[i][:DK])
            state = last[i] * state - moved
            state = jnp.concatenate([state[:DK], state[DK:] + change[i][DK:]], 0)
        total_ref[...] = state
        return carry

    lax.fori_loop(0, raw_ref.shape[0] // (CHUNK * GANG), gang, 0)


def join_kernel(place_ref, mine_ref, other_ref, prefix_ref, total_ref):
    place, core = place_ref[0], place_ref[1]
    row = lax.broadcasted_iota(jnp.int32, (DK + DV, DK), 0)
    col = lax.broadcasted_iota(jnp.int32, (DK + DV, DK), 1)
    state = jnp.where(row == col, 1.0, 0.0).astype(f32)
    prefix_ref[...] = state
    for j in range(8):
        piece = jnp.where(core == j % 2, mine_ref[j // 2], other_ref[j // 2])
        moved = mm_exact(state, piece[:DK])
        state = jnp.concatenate([moved[:DK], moved[DK:] + piece[DK:]], 0)

        @pl.when(place == j + 1)
        def _():
            prefix_ref[...] = state

    total_ref[...] = state


def read_kernel(place_ref, outer_ref, prefix_ref, reach_ref, own_ref, read_ref):
    place = place_ref[2]
    state = jnp.zeros((DV, DK), f32)
    for j in range(3):
        moved = mm_exact(state, outer_ref[j, :DK]) + outer_ref[j, DK:]
        state = jnp.where(j < place, moved, state)
    state = mm_exact(state, prefix_ref[:DK]) + prefix_ref[DK:]
    read_ref[...] = (mm(reach_ref[...], state, 1, 1) + own_ref[...]).astype(bf16)


def ring_gather(x, axis):
    size, me = lax.axis_size(axis), lax.axis_index(axis)
    out = jnp.zeros((size,) + x.shape, x.dtype)
    for shift in range(size):
        piece = x
        if shift:
            piece = lax.ppermute(x, axis, [(i, (i + shift) % size) for i in range(size)])
        out = lax.dynamic_update_index_in_dim(out, piece, lax.rem(me - shift + size, size), 0)
    return out


def shards(
    tokens, w_query, w_key, w_value, decay_proj, beta_proj, decay_rate, beta_bias, norm_gain
):
    local_rows = tokens.shape[0]
    streams = lax.axis_size("stream")
    head = lax.axis_index("stream")
    at_y, at_x, at_c = lax.axis_index("tm_0"), lax.axis_index("tm_1"), lax.axis_index("tm_2")
    vmem = pl.BlockSpec(memory_space=pltpu.VMEM)
    smem = pl.BlockSpec(memory_space=pltpu.SMEM)

    shares = 16
    rows = w_query.shape[0] // shares
    first = (at_y * 4 + at_x) * rows

    def share(w, width):
        return lax.dynamic_slice_in_dim(w, first, rows, 0).reshape(rows, HEADS, width)

    weights = jnp.concatenate(
        [
            share(w_query, DK),
            share(w_key, DK),
            share(w_value, DV),
            share(decay_proj, 1),
            share(beta_proj, 1),
            jnp.zeros((rows, HEADS, WIDE - 386), bf16),
        ],
        -1,
    ).transpose(1, 0, 2)
    all_tokens = lax.all_gather(tokens, "stream", axis=0, tiled=True)
    weights = lax.all_to_all(weights, "stream", split_axis=0, concat_axis=0, tiled=True)
    weights = ring_gather(ring_gather(weights, "tm_1"), "tm_0")
    weights = weights.transpose(2, 0, 1, 3, 4).reshape(streams * shares * rows, WIDE)

    raw = jnp.dot(all_tokens, weights, preferred_element_type=f32)
    block_rows = raw.shape[0]
    gates = jnp.stack(
        [
            lax.dynamic_index_in_dim(decay_rate, head, 0, False),
            lax.dynamic_index_in_dim(beta_bias, head, 0, False),
        ]
    )
    reach, own, total = pl.pallas_call(
        chunk_kernel,
        out_shape=(
            jax.ShapeDtypeStruct((block_rows, DK), bf16),
            jax.ShapeDtypeStruct((block_rows, DV), f32),
            jax.ShapeDtypeStruct((DK + DV, DK), f32),
        ),
        in_specs=[smem, vmem],
        out_specs=(vmem, vmem, vmem),
        compiler_params=pltpu.CompilerParams(vmem_limit_bytes=48 * 2**20),
    )(gates, raw)

    place = jnp.stack([at_x * 2 + at_c, at_c, at_y]).astype(jnp.int32)
    mine = lax.all_gather(total, "tm_1", axis=0)
    other = lax.ppermute(mine, "tm_2", [(0, 1), (1, 0)])
    prefix, subtotal = pl.pallas_call(
        join_kernel,
        out_shape=(jax.ShapeDtypeStruct((DK + DV, DK), f32),) * 2,
        in_specs=[smem, vmem, vmem],
        out_specs=(vmem, vmem),
    )(place, mine, other)
    outer = lax.all_gather(subtotal, "tm_0", axis=0)
    readout = pl.pallas_call(
        read_kernel,
        out_shape=jax.ShapeDtypeStruct((block_rows, DV), bf16),
        in_specs=[smem, vmem, vmem, vmem, vmem],
        out_specs=vmem,
        compiler_params=pltpu.CompilerParams(vmem_limit_bytes=32 * 2**20),
    )(place, outer, prefix, reach, own)
    returned = lax.all_to_all(readout, "stream", split_axis=0, concat_axis=1, tiled=True)
    head_read = returned.reshape(local_rows, HEADS, DV).astype(f32)
    normed = (
        head_read
        * lax.rsqrt(jnp.mean(head_read * head_read, -1, keepdims=True) + 1e-06)
        * norm_gain
    )
    return normed.reshape(local_rows, HEADS * DV).astype(bf16)


def solution(mesh):
    finer = Mesh(
        mesh.devices.reshape(4, 4, 2, mesh.shape["stream"]), ("tm_0", "tm_1", "tm_2", "stream")
    )
    return jax.shard_map(
        shards,
        mesh=finer,
        in_specs=(
            P(TM_STREAM, None),
            P("stream", None),
            P("stream", None),
            P("stream", None),
            P("stream", None),
            P("stream", None),
            P(),
            P(),
            P(),
        ),
        out_specs=P(TM_STREAM, None),
        check_vma=False,
    )
```

```python
import jax
import jax.numpy as jnp
from jax import lax
from jax.experimental import pallas as pl
from jax.experimental.pallas import tpu as pltpu
from jax.sharding import Mesh
from jax.sharding import PartitionSpec as P

HEADS = 16
DK = 128
DV = 128
CHUNK = 128
GANG = 8
SIDE = 4
MAP_ROWS = 272
SPLIT = ("tm_0", "tm_1", "tm_2", "zh", "zl")
STREAM = ("zh", "zl")
f32 = jnp.float32
bf16 = jnp.bfloat16


def mm(a, b, ca=1, cb=0):
    return lax.dot_general(
        a.astype(bf16), b.astype(bf16), (((ca,), (cb,)), ((), ())), preferred_element_type=f32
    )


def mm_exact(a, b, ca=1, cb=0):
    return lax.dot_general(
        a, b, (((ca,), (cb,)), ((), ())), precision=lax.Precision.HIGHEST, preferred_element_type=f32
    )


def chunk_kernel(gate_ref, *refs):
    raw_refs, (logit_ref, reach_ref, own_ref, total_ref) = refs[:SIDE], refs[SIDE:]
    chunks = raw_refs[0].shape[0] // CHUNK
    row = lax.broadcasted_iota(jnp.int32, (CHUNK, CHUNK), 0)
    col = lax.broadcasted_iota(jnp.int32, (CHUNK, CHUNK), 1)
    strict, inclusive = row > col, row >= col
    eye = jnp.where(row == col, 1.0, 0.0).astype(f32)
    ones_below = jnp.where(inclusive, 1.0, 0.0).astype(bf16)

    def below(size):
        return (
            (row // (2 * size) == col // (2 * size))
            & ((row // size) % 2 == 1)
            & ((col // size) % 2 == 0)
        )

    for step in range(SIDE * chunks // GANG):
        units = [divmod(step * GANG + i, chunks) for i in range(GANG)]
        starts = [j * CHUNK for _, j in units]
        each = range(GANG)
        q, k, v, beta, grow, scale_row, beta_row, tail, last, decay = ([] for _ in range(10))
        for i in each:
            raw_ref, mine = raw_refs[units[i][0]], units[i][0]
            rate, bias = gate_ref[2 * mine], gate_ref[2 * mine + 1]
            raw_q = raw_ref[pl.ds(starts[i], CHUNK), 0:128]
            raw_k = raw_ref[pl.ds(starts[i], CHUNK), 128:256]
            raw_v = raw_ref[pl.ds(starts[i], CHUNK), 256:384]
            logits = logit_ref[pl.ds(starts[i], CHUNK), :]
            q.append(
                (
                    raw_q
                    * lax.rsqrt(jnp.sum(raw_q * raw_q, -1, keepdims=True) + 1e-06)
                    * DK ** (-0.5)
                ).astype(bf16)
            )
            k.append(
                (raw_k * lax.rsqrt(jnp.sum(raw_k * raw_k, -1, keepdims=True) + 1e-06)).astype(bf16)
            )
            v.append(raw_v.astype(bf16))
            x = logits[:, 2 * mine : 2 * mine + 1]
            softplus = jnp.maximum(x, 0.0) + jnp.log1p(jnp.exp(-jnp.abs(x)))
            log_decay = (-rate * softplus).astype(bf16)
            strength = (1.0 / (1.0 + jnp.exp(-(logits[:, 2 * mine + 1 : 2 * mine + 2] + bias)))).astype(bf16).astype(f32)
            g = mm(ones_below, jnp.broadcast_to(log_decay, (CHUNK, CHUNK)))
            b = jnp.broadcast_to(strength, (CHUNK, CHUNK))
            turned = jnp.where(col < 64, g, b).T
            g_row, b_row = turned[0:1, :], turned[64:65, :]
            g_last = g_row[:, CHUNK - 1 : CHUNK]
            beta.append(b)
            grow.append(jnp.exp(g))
            beta_row.append(b_row)
            scale_row.append(b_row * jnp.exp(g_row))
            tail.append(jnp.exp(g_last - g))
            last.append(jnp.exp(g_last))
            decay.append(jnp.exp(jnp.where(inclusive, g - g_row, 0.0)))
        both = [mm(jnp.concatenate([q[i], k[i]], 0), k[i], 1, 1) for i in each]
        scores = [jnp.where(inclusive, both[i][:CHUNK] * decay[i], 0.0) for i in each]
        lower = [jnp.where(strict, beta[i] * decay[i] * both[i][CHUNK:], 0.0) for i in each]
        inverse = [eye - jnp.where(below(1), lower[i], 0.0) for i in each]
        for size in (2, 4, 8, 16, 32, 64):
            mask = below(size)
            inner = [mm(jnp.where(mask, lower[i], 0.0), inverse[i]) for i in each]
            inverse = [inverse[i] - mm(inverse[i], inner[i]) for i in each]
        rounded = [inverse[i].astype(bf16) for i in each]
        high = [lower[i].astype(bf16) for i in each]
        low = [(lower[i] - high[i].astype(f32)).astype(bf16) for i in each]
        rest = [
            eye - rounded[i].astype(f32) - mm(high[i], rounded[i]) - mm(low[i], rounded[i])
            for i in each
        ]
        inverse = [rounded[i].astype(f32) + mm(rounded[i], rest[i]) for i in each]
        w = [mm(inverse[i] * scale_row[i], k[i]) for i in each]
        u = [mm(inverse[i] * beta_row[i], v[i]) for i in each]
        wu = [jnp.concatenate([w[i], u[i]], 1) for i in each]
        tail2 = [jnp.concatenate([tail[i], tail[i]], 1) for i in each]
        change = [mm(wu[i] * tail2[i], k[i], 0, 0) for i in each]
        inside = [mm(scores[i], wu[i]) for i in each]
        reach = [grow[i] * q[i].astype(f32) - inside[i][:, :DK] for i in each]
        for i in each:
            mine, j = units[i]
            if j == 0:
                state = jnp.concatenate([eye, jnp.zeros((DV, DK), f32)], 0)
                kept = jnp.ones((1, 1), f32)
            out = mm(reach[i], state, 1, 1)
            reach_ref[mine, pl.ds(starts[i], CHUNK), :] = out[:, :DK].astype(bf16)
            own_ref[mine, pl.ds(starts[i], CHUNK), :] = out[:, DK:] + inside[i][:, DK:]
            moved = mm(state, change[i][:DK])
            state = last[i] * state - moved
            state = jnp.concatenate([state[:DK], state[DK:] + change[i][DK:]], 0)
            kept = kept * last[i]
            if j == chunks - 1:
                part = kept.astype(bf16).astype(f32)
                total_ref[mine, 0:DK, :] = (state[:DK] - kept * eye).astype(bf16)
                total_ref[mine, DK : DK + DV, :] = state[DK:].astype(bf16)
                total_ref[mine, DK + DV :, :] = jnp.concatenate(
                    [jnp.broadcast_to(part, (8, DK)), jnp.broadcast_to(kept - part, (8, DK))], 0
                ).astype(bf16)


def widen_map(packed, eye):
    kept = packed[DK + DV : DK + DV + 1].astype(f32) + packed[DK + DV + 8 : DK + DV + 9].astype(f32)
    return packed[:DK].astype(f32) + kept * eye, packed[DK : DK + DV].astype(f32)


def group_kernel(place_ref, *refs):
    part_refs, (prefix_ref, total_ref) = refs[:SIDE], refs[SIDE:]
    zh = place_ref[3]
    row = lax.broadcasted_iota(jnp.int32, (DK + DV, DK), 0)
    col = lax.broadcasted_iota(jnp.int32, (DK + DV, DK), 1)
    state = jnp.where(row == col, 1.0, 0.0).astype(f32)
    eye = state[:DK]
    for j in range(SIDE):
        prefix_ref[j] = state
        packed = part_refs[0][...]
        for shift in range(1, SIDE):
            packed = jnp.where(lax.rem(zh - shift + SIDE, SIDE) == j, part_refs[shift][...], packed)
        step, added = widen_map(packed, eye)
        moved = mm_exact(state, step)
        state = jnp.concatenate([moved[:DK], moved[DK:] + added], 0)
    total_ref[...] = state


def join_kernel(place_ref, mine_ref, other_ref, prefix_ref, total_ref):
    place, core = place_ref[0], place_ref[1]
    row = lax.broadcasted_iota(jnp.int32, (DK + DV, DK), 0)
    col = lax.broadcasted_iota(jnp.int32, (DK + DV, DK), 1)
    state = jnp.where(row == col, 1.0, 0.0).astype(f32)
    prefix_ref[...] = state
    for j in range(8):
        piece = jnp.where(core == j % 2, mine_ref[j // 2], other_ref[j // 2])
        moved = mm_exact(state, piece[:DK])
        state = jnp.concatenate([moved[:DK], moved[DK:] + piece[DK:]], 0)

        @pl.when(place == j + 1)
        def _():
            prefix_ref[...] = state

    total_ref[...] = state


def state_kernel(place_ref, outer_ref, prefix_ref, inner_ref, state_ref):
    place = place_ref[2]
    state = jnp.zeros((DV, DK), f32)
    for j in range(3):
        moved = mm_exact(state, outer_ref[j, :DK]) + outer_ref[j, DK:]
        state = jnp.where(j < place, moved, state)
    state = mm_exact(state, prefix_ref[:DK]) + prefix_ref[DK:]
    for j in range(SIDE):
        state_ref[j] = (mm_exact(state, inner_ref[j, :DK]) + inner_ref[j, DK:]).astype(bf16)


def read_kernel(place_ref, *refs):
    state_refs, (reach_ref, own_ref, read_ref) = refs[:SIDE], refs[SIDE:]
    at_y, zh = place_ref[2], place_ref[3]
    for k in range(SIDE):
        head = lax.rem(at_y - k + SIDE, SIDE)
        state = state_refs[0][...]
        for shift in range(1, SIDE):
            state = jnp.where(lax.rem(zh - shift + SIDE, SIDE) == head, state_refs[shift][...], state)
        read_ref[head] = (mm(reach_ref[k], state, 1, 1) + own_ref[k]).astype(bf16)


def shifted(x, axis, shift):
    size = lax.axis_size(axis)
    return lax.ppermute(x, axis, [(i, (i + shift) % size) for i in range(size)])


def ring_gather(x, axis):
    size, me = lax.axis_size(axis), lax.axis_index(axis)
    out = jnp.zeros((size,) + x.shape, x.dtype)
    for shift in range(size):
        piece = shifted(x, axis, shift) if shift else x
        out = lax.dynamic_update_index_in_dim(out, piece, lax.rem(me - shift + size, size), 0)
    return out


def shards(
    tokens, w_query, w_key, w_value, decay_proj, beta_proj, decay_rate, beta_bias, norm_gain
):
    local_rows = tokens.shape[0]
    at_y, at_x, at_c = lax.axis_index("tm_0"), lax.axis_index("tm_1"), lax.axis_index("tm_2")
    zh, zl = lax.axis_index("zh"), lax.axis_index("zl")
    vmem = pl.BlockSpec(memory_space=pltpu.VMEM)
    smem = pl.BlockSpec(memory_space=pltpu.SMEM)

    rows = w_query.shape[0] // 8
    first = (at_x * 2 + at_c) * rows

    def share(w):
        w = lax.dynamic_slice_in_dim(w, first, rows, 0).reshape(rows, SIDE, SIDE, DK)
        return lax.dynamic_index_in_dim(w, at_y, 2, False)

    weights = jnp.concatenate([share(w_query), share(w_key), share(w_value)], -1).transpose(1, 0, 2)
    run = lax.all_gather(tokens, "zl", axis=0, tiled=True)
    weights = lax.all_to_all(weights, "zl", split_axis=0, concat_axis=0, tiled=True)
    weights = ring_gather(weights, "zh")
    weights = ring_gather(weights, "tm_1")
    gates = jnp.concatenate([decay_proj, beta_proj], 1)
    gates = lax.all_gather(gates, "zl", axis=0, tiled=True)
    gates = lax.all_gather(gates, "zh", axis=0, tiled=True)
    heads = zl * SIDE + jnp.remainder(at_y - jnp.arange(SIDE), SIDE)
    wanted = jnp.stack([heads, heads + HEADS], 1).reshape(2 * SIDE)
    wanted = jnp.concatenate([wanted, jnp.full((128 - 2 * SIDE,), -1, wanted.dtype)])
    pick = (jnp.arange(2 * HEADS)[:, None] == wanted[None, :]).astype(bf16)
    gates = jnp.dot(gates, pick, preferred_element_type=f32).astype(bf16)
    logits = jnp.dot(run, gates, preferred_element_type=f32)
    both = jnp.concatenate([decay_rate, beta_bias])
    levels = jnp.sum(jnp.where(pick > 0, both[:, None], 0.0), 0)[: 2 * SIDE]

    raws = []
    for k in range(SIDE):
        own = shifted(weights, "tm_0", k) if k else weights
        other = shifted(own, "tm_2", 1)
        pair = jnp.stack([jnp.where(at_c == 0, own, other), jnp.where(at_c == 0, other, own)])
        matrix = pair.transpose(2, 3, 1, 0, 4, 5).reshape(tokens.shape[1], 3 * DK)
        raws.append(jnp.dot(run, matrix, preferred_element_type=f32))
    run_rows = run.shape[0]
    reach, own, total = pl.pallas_call(
        chunk_kernel,
        out_shape=(
            jax.ShapeDtypeStruct((SIDE, run_rows, DK), bf16),
            jax.ShapeDtypeStruct((SIDE, run_rows, DV), f32),
            jax.ShapeDtypeStruct((SIDE, MAP_ROWS, DK), bf16),
        ),
        in_specs=[smem] + [vmem] * 5,
        out_specs=(vmem, vmem, vmem),
        compiler_params=pltpu.CompilerParams(vmem_limit_bytes=48 * 2**20),
    )(levels, *raws, logits)

    place = jnp.stack([at_x * 2 + at_c, at_c, at_y, zh]).astype(jnp.int32)
    parts = []
    for shift in range(SIDE):
        sent = lax.dynamic_index_in_dim(total, jnp.remainder(at_y - zh - shift, SIDE), 0, False)
        parts.append(shifted(sent, "zh", shift) if shift else sent)
    inner, block = pl.pallas_call(
        group_kernel,
        out_shape=(
            jax.ShapeDtypeStruct((SIDE, DK + DV, DK), f32),
            jax.ShapeDtypeStruct((DK + DV, DK), f32),
        ),
        in_specs=[smem] + [vmem] * SIDE,
        out_specs=(vmem, vmem),
    )(place, *parts)
    mine = lax.all_gather(block, "tm_1", axis=0)
    other = lax.ppermute(mine, "tm_2", [(0, 1), (1, 0)])
    prefix, subtotal = pl.pallas_call(
        join_kernel,
        out_shape=(jax.ShapeDtypeStruct((DK + DV, DK), f32),) * 2,
        in_specs=[smem, vmem, vmem],
        out_specs=(vmem, vmem),
    )(place, mine, other)
    outer = lax.all_gather(subtotal, "tm_0", axis=0)
    states = pl.pallas_call(
        state_kernel,
        out_shape=jax.ShapeDtypeStruct((SIDE, DV, DK), bf16),
        in_specs=[smem] + [vmem] * 3,
        out_specs=vmem,
    )(place, outer, prefix, inner)
    arrived = []
    for shift in range(SIDE):
        sent = lax.dynamic_index_in_dim(states, jnp.remainder(zh + shift, SIDE), 0, False)
        arrived.append(shifted(sent, "zh", shift) if shift else sent)
    readout = pl.pallas_call(
        read_kernel,
        out_shape=jax.ShapeDtypeStruct((SIDE, run_rows, DV), bf16),
        in_specs=[smem] + [vmem] * (SIDE + 2),
        out_specs=vmem,
        compiler_params=pltpu.CompilerParams(vmem_limit_bytes=32 * 2**20),
    )(place, *arrived, reach, own)
    returned = lax.all_to_all(
        readout.reshape(SIDE, SIDE, local_rows, DV), "zl", split_axis=1, concat_axis=0, tiled=True
    )
    head_read = returned.reshape(HEADS, local_rows, DV).transpose(1, 0, 2).astype(f32)
    normed = (
        head_read
        * lax.rsqrt(jnp.mean(head_read * head_read, -1, keepdims=True) + 1e-06)
        * norm_gain
    )
    return normed.reshape(local_rows, HEADS * DV).astype(bf16)


def solution(mesh):
    finer = Mesh(mesh.devices.reshape(4, 4, 2, SIDE, SIDE), SPLIT)
    return jax.shard_map(
        shards,
        mesh=finer,
        in_specs=(
            P(SPLIT, None),
            P(STREAM, None),
            P(STREAM, None),
            P(STREAM, None),
            P(STREAM, None),
            P(STREAM, None),
            P(),
            P(),
            P(),
        ),
        out_specs=P(SPLIT, None),
        check_vma=False,
    )
```

```python
import jax
import jax.numpy as jnp
from jax import lax
from jax.experimental import pallas as pl
from jax.experimental.pallas import tpu as pltpu
from jax.sharding import Mesh
from jax.sharding import PartitionSpec as P

HEADS = 16
DK = 128
DV = 128
CHUNK = 128
GANG = 8
SIDE = 4
MAP_ROWS = 272
SPLIT = ("tm_0", "tm_1", "tm_2", "zh", "zl")
STREAM = ("zh", "zl")
f32 = jnp.float32
bf16 = jnp.bfloat16


def mm(a, b, ca=1, cb=0):
    return lax.dot_general(
        a.astype(bf16), b.astype(bf16), (((ca,), (cb,)), ((), ())), preferred_element_type=f32
    )


def mm_exact(a, b, ca=1, cb=0):
    return lax.dot_general(
        a, b, (((ca,), (cb,)), ((), ())), precision=lax.Precision.HIGHEST, preferred_element_type=f32
    )


def chunk_kernel(place_ref, rate_ref, bias_ref, *refs):
    token_ref, first_ref, own_refs, other_refs = refs[0], refs[1], refs[2 : SIDE + 1], refs[SIDE + 1 : 2 * SIDE + 1]
    reach_ref, own_ref, total_ref, matrix_ref, raw_ref, logit_ref = refs[2 * SIDE + 1 :]
    core, at_y, group = place_ref[1], place_ref[2], place_ref[4]
    chunks = token_ref.shape[0] // CHUNK
    places = [lax.rem(place_ref[5] - x + SIDE, SIDE) for x in range(SIDE)]
    lane = lax.broadcasted_iota(jnp.int32, (1, 128), 1)
    keep = [jnp.where((lane // SIDE) % 2 == c, 1.0, 0.0).astype(bf16) for c in range(2)]

    def gate_rows(z, carry):
        for x in range(SIDE):
            for c in range(2):
                at = pl.ds(pl.multiple_of(z * 128 + (places[x] * 2 + c) * 16, 16), 16)
                matrix_ref[at, 0:128] = first_ref[x, z, :, 384:512] * keep[c]
        return carry

    lax.fori_loop(0, first_ref.shape[1], gate_rows, 0)
    logit_ref[...] = jnp.dot(token_ref[...], matrix_ref[:, 0:128], preferred_element_type=f32)

    for k in range(SIDE):

        def head_rows(z, carry, k=k):
            for x in range(SIDE):
                mine = own_refs[k - 1][x, z] if k else first_ref[x, z, :, 0:384]
                other = other_refs[k][x, z]
                for c in range(2):
                    at = pl.ds(pl.multiple_of(z * 128 + (places[x] * 2 + c) * 16, 16), 16)
                    matrix_ref[at, :] = jnp.where(core == c, mine, other)
            return carry

        lax.fori_loop(0, first_ref.shape[1], head_rows, 0)
        raw_ref[k] = jnp.dot(token_ref[...], matrix_ref[...], preferred_element_type=f32)

    row = lax.broadcasted_iota(jnp.int32, (CHUNK, CHUNK), 0)
    col = lax.broadcasted_iota(jnp.int32, (CHUNK, CHUNK), 1)
    strict, inclusive = row > col, row >= col
    eye = jnp.where(row == col, 1.0, 0.0).astype(f32)
    ones_below = jnp.where(inclusive, 1.0, 0.0).astype(bf16)

    def below(size):
        return (
            (row // (2 * size) == col // (2 * size))
            & ((row // size) % 2 == 1)
            & ((col // size) % 2 == 0)
        )

    for step in range(SIDE * chunks // GANG):
        units = [divmod(step * GANG + i, chunks) for i in range(GANG)]
        starts = [j * CHUNK for _, j in units]
        each = range(GANG)
        q, k, v, beta, grow, scale_row, beta_row, tail, last, decay = ([] for _ in range(10))
        for i in each:
            mine = units[i][0]
            head = lax.rem(at_y - mine + SIDE, SIDE)
            rate, bias = rate_ref[group * SIDE + head], bias_ref[group * SIDE + head]
            raw_q = raw_ref[mine, pl.ds(starts[i], CHUNK), 0:128]
            raw_k = raw_ref[mine, pl.ds(starts[i], CHUNK), 128:256]
            raw_v = raw_ref[mine, pl.ds(starts[i], CHUNK), 256:384]
            logits = logit_ref[pl.ds(starts[i], CHUNK), :]
            q.append(
                (
                    raw_q
                    * lax.rsqrt(jnp.sum(raw_q * raw_q, -1, keepdims=True) + 1e-06)
                    * DK ** (-0.5)
                ).astype(bf16)
            )
            k.append(
                (raw_k * lax.rsqrt(jnp.sum(raw_k * raw_k, -1, keepdims=True) + 1e-06)).astype(bf16)
            )
            v.append(raw_v.astype(bf16))
            of_head = (lane % SIDE == head) & (lane < 4 * SIDE)
            x = jnp.sum(jnp.where(of_head & (lane < 2 * SIDE), logits, 0.0), -1, keepdims=True)
            y = jnp.sum(jnp.where(of_head & (lane >= 2 * SIDE), logits, 0.0), -1, keepdims=True)
            softplus = jnp.maximum(x, 0.0) + jnp.log1p(jnp.exp(-jnp.abs(x)))
            log_decay = (-rate * softplus).astype(bf16)
            strength = (1.0 / (1.0 + jnp.exp(-(y + bias)))).astype(bf16).astype(f32)
            g = mm(ones_below, jnp.broadcast_to(log_decay, (CHUNK, CHUNK)))
            b = jnp.broadcast_to(strength, (CHUNK, CHUNK))
            turned = jnp.where(col < 64, g, b).T
            g_row, b_row = turned[0:1, :], turned[64:65, :]
            g_last = g_row[:, CHUNK - 1 : CHUNK]
            beta.append(b)
            grow.append(jnp.exp(g))
            beta_row.append(b_row)
            scale_row.append(b_row * jnp.exp(g_row))
            tail.append(jnp.exp(g_last - g))
            last.append(jnp.exp(g_last))
            decay.append(jnp.exp(jnp.where(inclusive, g - g_row, 0.0)))
        both = [mm(jnp.concatenate([q[i], k[i]], 0), k[i], 1, 1) for i in each]
        scores = [jnp.where(inclusive, both[i][:CHUNK] * decay[i], 0.0) for i in each]
        lower = [jnp.where(strict, beta[i] * decay[i] * both[i][CHUNK:], 0.0) for i in each]
        inverse = [eye - jnp.where(below(1), lower[i], 0.0) for i in each]
        for size in (2, 4, 8, 16, 32, 64):
            mask = below(size)
            inner = [mm(jnp.where(mask, lower[i], 0.0), inverse[i]) for i in each]
            inverse = [inverse[i] - mm(inverse[i], inner[i]) for i in each]
        rounded = [inverse[i].astype(bf16) for i in each]
        high = [lower[i].astype(bf16) for i in each]
        low = [(lower[i] - high[i].astype(f32)).astype(bf16) for i in each]
        rest = [
            eye - rounded[i].astype(f32) - mm(high[i], rounded[i]) - mm(low[i], rounded[i])
            for i in each
        ]
        inverse = [rounded[i].astype(f32) + mm(rounded[i], rest[i]) for i in each]
        w = [mm(inverse[i] * scale_row[i], k[i]) for i in each]
        u = [mm(inverse[i] * beta_row[i], v[i]) for i in each]
        wu = [jnp.concatenate([w[i], u[i]], 1) for i in each]
        tail2 = [jnp.concatenate([tail[i], tail[i]], 1) for i in each]
        change = [mm(wu[i] * tail2[i], k[i], 0, 0) for i in each]
        inside = [mm(scores[i], wu[i]) for i in each]
        reach = [grow[i] * q[i].astype(f32) - inside[i][:, :DK] for i in each]
        for i in each:
            mine, j = units[i]
            head = lax.rem(at_y - mine + SIDE, SIDE)
            if j == 0:
                state = jnp.concatenate([eye, jnp.zeros((DV, DK), f32)], 0)
                kept = jnp.ones((1, 1), f32)
            out = mm(reach[i], state, 1, 1)
            reach_ref[head, pl.ds(starts[i], CHUNK), :] = out[:, :DK].astype(bf16)
            own_ref[head, pl.ds(starts[i], CHUNK), :] = out[:, DK:] + inside[i][:, DK:]
            moved = mm(state, change[i][:DK])
            state = last[i] * state - moved
            state = jnp.concatenate([state[:DK], state[DK:] + change[i][DK:]], 0)
            kept = kept * last[i]
            if j == chunks - 1:
                part = kept.astype(bf16).astype(f32)
                total_ref[head, 0:DK, :] = (state[:DK] - kept * eye).astype(bf16)
                total_ref[head, DK : DK + DV, :] = state[DK:].astype(bf16)
                total_ref[head, DK + DV :, :] = jnp.concatenate(
                    [jnp.broadcast_to(part, (8, DK)), jnp.broadcast_to(kept - part, (8, DK))], 0
                ).astype(bf16)


def widen_map(packed, eye):
    kept = packed[DK + DV : DK + DV + 1].astype(f32) + packed[DK + DV + 8 : DK + DV + 9].astype(f32)
    return packed[:DK].astype(f32) + kept * eye, packed[DK : DK + DV].astype(f32)


def group_kernel(part_ref, prefix_ref, total_ref):
    row = lax.broadcasted_iota(jnp.int32, (DK + DV, DK), 0)
    col = lax.broadcasted_iota(jnp.int32, (DK + DV, DK), 1)
    state = jnp.where(row == col, 1.0, 0.0).astype(f32)
    eye = state[:DK]
    for j in range(SIDE):
        prefix_ref[j] = state
        step, added = widen_map(part_ref[j], eye)
        moved = mm_exact(state, step)
        state = jnp.concatenate([moved[:DK], moved[DK:] + added], 0)
    total_ref[...] = state


def join_kernel(place_ref, mine_ref, other_ref, prefix_ref, total_ref):
    place, core = place_ref[0], place_ref[1]
    row = lax.broadcasted_iota(jnp.int32, (DK + DV, DK), 0)
    col = lax.broadcasted_iota(jnp.int32, (DK + DV, DK), 1)
    state = jnp.where(row == col, 1.0, 0.0).astype(f32)
    prefix_ref[...] = state
    for j in range(8):
        piece = jnp.where(core == j % 2, mine_ref[j // 2], other_ref[j // 2])
        moved = mm_exact(state, piece[:DK])
        state = jnp.concatenate([moved[:DK], moved[DK:] + piece[DK:]], 0)

        @pl.when(place == j + 1)
        def _():
            prefix_ref[...] = state

    total_ref[...] = state


def state_kernel(place_ref, outer_ref, prefix_ref, inner_ref, state_ref):
    place = place_ref[2]
    state = jnp.zeros((DV, DK), f32)
    for j in range(3):
        moved = mm_exact(state, outer_ref[j, :DK]) + outer_ref[j, DK:]
        state = jnp.where(j < place, moved, state)
    state = mm_exact(state, prefix_ref[:DK]) + prefix_ref[DK:]
    for j in range(SIDE):
        state_ref[j] = (mm_exact(state, inner_ref[j, :DK]) + inner_ref[j, DK:]).astype(bf16)


def read_kernel(state_ref, reach_ref, own_ref, read_ref):
    for head in range(SIDE):
        read_ref[head] = (mm(reach_ref[head], state_ref[head], 1, 1) + own_ref[head]).astype(bf16)


def shifted(x, axis, shift):
    size = lax.axis_size(axis)
    return lax.ppermute(x, axis, [(i, (i + shift) % size) for i in range(size)])


def shards(
    tokens, w_query, w_key, w_value, decay_proj, beta_proj, decay_rate, beta_bias, norm_gain
):
    local_rows = tokens.shape[0]
    at_y, at_x, at_c = lax.axis_index("tm_0"), lax.axis_index("tm_1"), lax.axis_index("tm_2")
    zh, zl = lax.axis_index("zh"), lax.axis_index("zl")
    vmem = pl.BlockSpec(memory_space=pltpu.VMEM)
    smem = pl.BlockSpec(memory_space=pltpu.SMEM)

    rows = w_query.shape[0] // 8
    first = (at_x * 2 + at_c) * rows

    def share(w):
        w = lax.dynamic_slice_in_dim(w, first, rows, 0).reshape(rows, SIDE, SIDE, DK)
        return lax.dynamic_index_in_dim(w, at_y, 2, False)

    def gate_share(w):
        w = lax.dynamic_slice_in_dim(w, at_x * 2 * rows, 2 * rows, 0).reshape(2, rows, SIDE, SIDE)
        return w.transpose(1, 2, 0, 3).reshape(rows, SIDE, 2 * SIDE)

    weights = jnp.concatenate(
        [
            share(w_query),
            share(w_key),
            share(w_value),
            gate_share(decay_proj),
            gate_share(beta_proj),
            jnp.zeros((rows, SIDE, 128 - 4 * SIDE), bf16),
        ],
        -1,
    ).transpose(1, 0, 2)
    weights = jnp.broadcast_to(weights[None], (SIDE,) + weights.shape)
    weights = weights.reshape((SIDE * SIDE,) + weights.shape[2:])
    run = lax.all_gather(tokens, "zl", axis=0, tiled=True)
    weights = lax.all_to_all(weights, STREAM, split_axis=0, concat_axis=0, tiled=True)
    first = jnp.stack([weights] + [shifted(weights, "tm_1", k) for k in range(1, SIDE)])
    narrow = first[..., : 3 * DK]
    mine = [narrow] + [shifted(narrow, "tm_0", k) for k in range(1, SIDE)]
    others = [shifted(a, "tm_2", 1) for a in mine]
    place = jnp.stack([at_x * 2 + at_c, at_c, at_y, zh, zl, at_x]).astype(jnp.int32)
    run_rows, features = run.shape
    reach, own, total = pl.pallas_call(
        chunk_kernel,
        out_shape=(
            jax.ShapeDtypeStruct((SIDE, run_rows, DK), bf16),
            jax.ShapeDtypeStruct((SIDE, run_rows, DV), f32),
            jax.ShapeDtypeStruct((SIDE, MAP_ROWS, DK), bf16),
        ),
        in_specs=[smem] * 3 + [vmem] * (2 * SIDE + 1),
        out_specs=(vmem, vmem, vmem),
        scratch_shapes=[
            pltpu.VMEM((features, 3 * DK), bf16),
            pltpu.VMEM((SIDE, run_rows, 3 * DK), f32),
            pltpu.VMEM((run_rows, 128), f32),
        ],
        compiler_params=pltpu.CompilerParams(vmem_limit_bytes=56 * 2**20),
    )(place, decay_rate, beta_bias, run, first, *mine[1:], *others)

    parts = lax.all_to_all(total, "zh", split_axis=0, concat_axis=0, tiled=True)
    inner, block = pl.pallas_call(
        group_kernel,
        out_shape=(
            jax.ShapeDtypeStruct((SIDE, DK + DV, DK), f32),
            jax.ShapeDtypeStruct((DK + DV, DK), f32),
        ),
        in_specs=[vmem],
        out_specs=(vmem, vmem),
    )(parts)
    mine = lax.all_gather(block, "tm_1", axis=0)
    other = lax.ppermute(mine, "tm_2", [(0, 1), (1, 0)])
    prefix, subtotal = pl.pallas_call(
        join_kernel,
        out_shape=(jax.ShapeDtypeStruct((DK + DV, DK), f32),) * 2,
        in_specs=[smem, vmem, vmem],
        out_specs=(vmem, vmem),
    )(place, mine, other)
    outer = lax.all_gather(subtotal, "tm_0", axis=0)
    states = pl.pallas_call(
        state_kernel,
        out_shape=jax.ShapeDtypeStruct((SIDE, DV, DK), bf16),
        in_specs=[smem] + [vmem] * 3,
        out_specs=vmem,
    )(place, outer, prefix, inner)
    states = lax.all_to_all(states, "zh", split_axis=0, concat_axis=0, tiled=True)
    readout = pl.pallas_call(
        read_kernel,
        out_shape=jax.ShapeDtypeStruct((SIDE, run_rows, DV), bf16),
        in_specs=[vmem] * 3,
        out_specs=vmem,
        compiler_params=pltpu.CompilerParams(vmem_limit_bytes=32 * 2**20),
    )(states, reach, own)
    returned = lax.all_to_all(
        readout.reshape(SIDE, SIDE, local_rows, DV), "zl", split_axis=1, concat_axis=0, tiled=True
    )
    head_read = returned.reshape(HEADS, local_rows, DV).transpose(1, 0, 2).astype(f32)
    normed = (
        head_read
        * lax.rsqrt(jnp.mean(head_read * head_read, -1, keepdims=True) + 1e-06)
        * norm_gain
    )
    return normed.reshape(local_rows, HEADS * DV).astype(bf16)


def solution(mesh):
    finer = Mesh(mesh.devices.reshape(4, 4, 2, SIDE, SIDE), SPLIT)
    return jax.shard_map(
        shards,
        mesh=finer,
        in_specs=(
            P(SPLIT, None),
            P(STREAM, None),
            P(STREAM, None),
            P(STREAM, None),
            P(STREAM, None),
            P(STREAM, None),
            P(),
            P(),
            P(),
        ),
        out_specs=P(SPLIT, None),
        check_vma=False,
    )
```

```python
import jax
import jax.numpy as jnp
from jax import lax
from jax.experimental import pallas as pl
from jax.experimental.pallas import tpu as pltpu
from jax.sharding import Mesh
from jax.sharding import PartitionSpec as P

HEADS = 16
DK = 128
DV = 128
CHUNK = 128
GANG = 8
WIDE = 512
MAP_ROWS = 272
PLANE = ("tm_0", "tm_1", "tm_2")
TM_STREAM = ("tm_0", "tm_1", "tm_2", "stream")
f32 = jnp.float32
bf16 = jnp.bfloat16


def mm(a, b, ca=1, cb=0):
    return lax.dot_general(
        a.astype(bf16), b.astype(bf16), (((ca,), (cb,)), ((), ())), preferred_element_type=f32
    )


def chunk_kernel(
    head_ref,
    rate_ref,
    bias_ref,
    token_ref,
    weight_ref,
    reach_ref,
    own_ref,
    total_ref,
    raw_ref,
    state_ref,
):
    rate, bias = rate_ref[head_ref[0]], bias_ref[head_ref[0]]
    raw_ref[...] = jnp.dot(token_ref[...], weight_ref[...], preferred_element_type=f32)
    row = lax.broadcasted_iota(jnp.int32, (CHUNK, CHUNK), 0)
    col = lax.broadcasted_iota(jnp.int32, (CHUNK, CHUNK), 1)
    strict, inclusive = row > col, row >= col
    eye = jnp.where(row == col, 1.0, 0.0).astype(f32)
    ones_below = jnp.where(inclusive, 1.0, 0.0).astype(bf16)

    @pl.when(pl.program_id(0) == 0)
    def _():
        state_ref[0:DK, :] = eye
        state_ref[DK : DK + DV, :] = jnp.zeros((DV, DK), f32)
        state_ref[DK + DV :, :] = jnp.ones((8, DK), f32)

    def below(size):
        return (
            (row // (2 * size) == col // (2 * size))
            & ((row // size) % 2 == 1)
            & ((col // size) % 2 == 0)
        )

    def gang(step, carry):
        starts = [pl.multiple_of((step * GANG + i) * CHUNK, CHUNK) for i in range(GANG)]
        each = range(GANG)
        q, k, v, beta, grow, scale_row, beta_row, tail, last, decay = ([] for _ in range(10))
        for i in each:
            raw_q = raw_ref[pl.ds(starts[i], CHUNK), 0:128]
            raw_k = raw_ref[pl.ds(starts[i], CHUNK), 128:256]
            raw_v = raw_ref[pl.ds(starts[i], CHUNK), 256:384]
            logits = raw_ref[pl.ds(starts[i], CHUNK), 384:512]
            q.append(
                (
                    raw_q
                    * lax.rsqrt(jnp.sum(raw_q * raw_q, -1, keepdims=True) + 1e-06)
                    * DK ** (-0.5)
                ).astype(bf16)
            )
            k.append(
                (raw_k * lax.rsqrt(jnp.sum(raw_k * raw_k, -1, keepdims=True) + 1e-06)).astype(bf16)
            )
            v.append(raw_v.astype(bf16))
            x = logits[:, 0:1]
            softplus = jnp.maximum(x, 0.0) + jnp.log1p(jnp.exp(-jnp.abs(x)))
            log_decay = (-rate * softplus).astype(bf16)
            strength = (1.0 / (1.0 + jnp.exp(-(logits[:, 1:2] + bias)))).astype(bf16).astype(f32)
            g = mm(ones_below, jnp.broadcast_to(log_decay, (CHUNK, CHUNK)))
            b = jnp.broadcast_to(strength, (CHUNK, CHUNK))
            turned = jnp.where(col < 64, g, b).T
            g_row, b_row = turned[0:1, :], turned[64:65, :]
            g_last = g_row[:, CHUNK - 1 : CHUNK]
            beta.append(b)
            grow.append(jnp.exp(g))
            beta_row.append(b_row)
            scale_row.append(b_row * jnp.exp(g_row))
            tail.append(jnp.exp(g_last - g))
            last.append(jnp.exp(g_last))
            decay.append(jnp.exp(jnp.where(inclusive, g - g_row, 0.0)))
        both = [mm(jnp.concatenate([q[i], k[i]], 0), k[i], 1, 1) for i in each]
        scores = [jnp.where(inclusive, both[i][:CHUNK] * decay[i], 0.0) for i in each]
        lower = [jnp.where(strict, beta[i] * decay[i] * both[i][CHUNK:], 0.0) for i in each]
        inverse = [eye - jnp.where(below(1), lower[i], 0.0) for i in each]
        for size in (2, 4, 8, 16, 32, 64):
            mask = below(size)
            inner = [mm(jnp.where(mask, lower[i], 0.0), inverse[i]) for i in each]
            inverse = [inverse[i] - mm(inverse[i], inner[i]) for i in each]
        rounded = [inverse[i].astype(bf16) for i in each]
        high = [lower[i].astype(bf16) for i in each]
        low = [(lower[i] - high[i].astype(f32)).astype(bf16) for i in each]
        rest = [
            eye - rounded[i].astype(f32) - mm(high[i], rounded[i]) - mm(low[i], rounded[i])
            for i in each
        ]
        inverse = [rounded[i].astype(f32) + mm(rounded[i], rest[i]) for i in each]
        w = [mm(inverse[i] * scale_row[i], k[i]) for i in each]
        u = [mm(inverse[i] * beta_row[i], v[i]) for i in each]
        wu = [jnp.concatenate([w[i], u[i]], 1) for i in each]
        tail2 = [jnp.concatenate([tail[i], tail[i]], 1) for i in each]
        change = [mm(wu[i] * tail2[i], k[i], 0, 0) for i in each]
        inside = [mm(scores[i], wu[i]) for i in each]
        reach = [grow[i] * q[i].astype(f32) - inside[i][:, :DK] for i in each]
        state, kept = state_ref[0 : DK + DV, :], state_ref[DK + DV :, :]
        for i in each:
            out = mm(reach[i], state, 1, 1)
            reach_ref[pl.ds(starts[i], CHUNK), :] = out[:, :DK].astype(bf16)
            own_ref[pl.ds(starts[i], CHUNK), :] = out[:, DK:] + inside[i][:, DK:]
            moved = mm(state, change[i][:DK])
            state = last[i] * state - moved
            state = jnp.concatenate([state[:DK], state[DK:] + change[i][DK:]], 0)
            kept = last[i] * kept
        state_ref[0 : DK + DV, :] = state
        state_ref[DK + DV :, :] = kept
        return carry

    lax.fori_loop(0, raw_ref.shape[0] // (CHUNK * GANG), gang, 0)

    @pl.when(pl.program_id(0) == pl.num_programs(0) - 1)
    def _():
        kept = state_ref[DK + DV :, :]
        part = kept.astype(bf16).astype(f32)
        total_ref[0:DK, :] = (state_ref[0:DK, :] - kept[0:1] * eye).astype(bf16)
        total_ref[DK : DK + DV, :] = state_ref[DK : DK + DV, :].astype(bf16)
        total_ref[DK + DV :, :] = jnp.concatenate([part, kept - part], 0).astype(bf16)


def read_kernel(place_ref, map_ref, reach_ref, own_ref, read_ref):
    def one(j, state):
        kept = map_ref[j, DK + DV : MAP_ROWS, :].astype(f32)
        kept = kept[0:1] + kept[8:9]
        return kept * state + mm(state, map_ref[j, 0:DK, :]) + map_ref[j, DK : DK + DV, :].astype(f32)

    state = lax.fori_loop(0, place_ref[0], one, jnp.zeros((DV, DK), f32))
    read_ref[...] = (mm(reach_ref[...], state, 1, 1) + own_ref[...]).astype(bf16)


def shards(
    tokens, w_query, w_key, w_value, decay_proj, beta_proj, decay_rate, beta_bias, norm_gain
):
    local_rows = tokens.shape[0]
    streams = lax.axis_size("stream")
    head = lax.axis_index("stream")
    at_y, at_x, at_c = lax.axis_index("tm_0"), lax.axis_index("tm_1"), lax.axis_index("tm_2")
    vmem = pl.BlockSpec(memory_space=pltpu.VMEM)
    smem = pl.BlockSpec(memory_space=pltpu.SMEM)

    shares = 16
    rows = w_query.shape[0] // shares
    first = (at_y * 4 + at_x) * rows

    def share(w, width):
        return lax.dynamic_slice_in_dim(w, first, rows, 0).reshape(rows, HEADS, width)

    weights = jnp.concatenate(
        [
            share(w_query, DK),
            share(w_key, DK),
            share(w_value, DV),
            share(decay_proj, 1),
            share(beta_proj, 1),
            jnp.zeros((rows, HEADS, WIDE - 386), bf16),
        ],
        -1,
    ).transpose(1, 0, 2)
    all_tokens = lax.all_gather(tokens, "stream", axis=0, tiled=True)
    weights = lax.all_to_all(weights, "stream", split_axis=0, concat_axis=0, tiled=True)
    weights = jnp.broadcast_to(weights[None], (shares,) + weights.shape)
    weights = lax.all_to_all(weights, ("tm_0", "tm_1"), split_axis=0, concat_axis=0, tiled=True)
    weights = weights.transpose(1, 0, 2, 3).reshape(streams * shares * rows, WIDE)

    block_rows, features = all_tokens.shape
    stretch = CHUNK * GANG
    reach, own, total = pl.pallas_call(
        chunk_kernel,
        out_shape=(
            jax.ShapeDtypeStruct((block_rows, DK), bf16),
            jax.ShapeDtypeStruct((block_rows, DV), f32),
            jax.ShapeDtypeStruct((MAP_ROWS, DK), bf16),
        ),
        grid=(block_rows // stretch,),
        in_specs=[
            smem,
            smem,
            smem,
            pl.BlockSpec((stretch, features), lambda i: (i, 0)),
            pl.BlockSpec((features, WIDE), lambda i: (0, 0)),
        ],
        out_specs=(
            pl.BlockSpec((stretch, DK), lambda i: (i, 0)),
            pl.BlockSpec((stretch, DV), lambda i: (i, 0)),
            pl.BlockSpec((MAP_ROWS, DK), lambda i: (0, 0)),
        ),
        scratch_shapes=[
            pltpu.VMEM((stretch, WIDE), f32),
            pltpu.VMEM((DK + DV + 8, DK), f32),
        ],
        compiler_params=pltpu.CompilerParams(vmem_limit_bytes=48 * 2**20),
    )(head.reshape(1).astype(jnp.int32), decay_rate, beta_bias, all_tokens, weights)

    runs = 32
    maps = jnp.broadcast_to(total[None], (runs,) + total.shape)
    maps = lax.all_to_all(maps, PLANE, split_axis=0, concat_axis=0, tiled=True)
    place = ((at_y * 4 + at_x) * 2 + at_c).reshape(1).astype(jnp.int32)
    readout = pl.pallas_call(
        read_kernel,
        out_shape=jax.ShapeDtypeStruct((block_rows, DV), bf16),
        in_specs=[smem, vmem, vmem, vmem],
        out_specs=vmem,
        compiler_params=pltpu.CompilerParams(vmem_limit_bytes=32 * 2**20),
    )(place, maps, reach, own)
    returned = lax.all_to_all(readout, "stream", split_axis=0, concat_axis=1, tiled=True)
    head_read = returned.reshape(local_rows, HEADS, DV).astype(f32)
    normed = (
        head_read
        * lax.rsqrt(jnp.mean(head_read * head_read, -1, keepdims=True) + 1e-06)
        * norm_gain
    )
    return normed.reshape(local_rows, HEADS * DV).astype(bf16)


def solution(mesh):
    finer = Mesh(
        mesh.devices.reshape(4, 4, 2, mesh.shape["stream"]), ("tm_0", "tm_1", "tm_2", "stream")
    )
    return jax.shard_map(
        shards,
        mesh=finer,
        in_specs=(
            P(TM_STREAM, None),
            P("stream", None),
            P("stream", None),
            P("stream", None),
            P("stream", None),
            P("stream", None),
            P(),
            P(),
            P(),
        ),
        out_specs=P(TM_STREAM, None),
        check_vma=False,
    )
```

```python
import jax
import jax.numpy as jnp
from jax import lax
from jax.experimental import pallas as pl
from jax.experimental.pallas import tpu as pltpu
from jax.sharding import Mesh
from jax.sharding import PartitionSpec as P

HEADS = 16
DK = 128
DV = 128
CHUNK = 128
GANG = 8
WIDE = 512
MAP_ROWS = 272
TM_STREAM = ("tm_0", "tm_1", "tm_2", "stream")
f32 = jnp.float32
bf16 = jnp.bfloat16


def mm(a, b, ca=1, cb=0):
    return lax.dot_general(
        a.astype(bf16), b.astype(bf16), (((ca,), (cb,)), ((), ())), preferred_element_type=f32
    )


def chunk_kernel(
    head_ref,
    rate_ref,
    bias_ref,
    token_ref,
    weight_ref,
    reach_ref,
    own_ref,
    total_ref,
    raw_ref,
    state_ref,
):
    rate, bias = rate_ref[head_ref[0]], bias_ref[head_ref[0]]
    raw_ref[...] = jnp.dot(token_ref[...], weight_ref[...], preferred_element_type=f32)
    row = lax.broadcasted_iota(jnp.int32, (CHUNK, CHUNK), 0)
    col = lax.broadcasted_iota(jnp.int32, (CHUNK, CHUNK), 1)
    strict, inclusive = row > col, row >= col
    eye = jnp.where(row == col, 1.0, 0.0).astype(f32)
    ones_below = jnp.where(inclusive, 1.0, 0.0).astype(bf16)

    @pl.when(pl.program_id(0) == 0)
    def _():
        state_ref[0:DK, :] = eye
        state_ref[DK : DK + DV, :] = jnp.zeros((DV, DK), f32)
        state_ref[DK + DV :, :] = jnp.ones((8, DK), f32)

    def below(size):
        return (
            (row // (2 * size) == col // (2 * size))
            & ((row // size) % 2 == 1)
            & ((col // size) % 2 == 0)
        )

    def gang(step, carry):
        starts = [pl.multiple_of((step * GANG + i) * CHUNK, CHUNK) for i in range(GANG)]
        each = range(GANG)
        q, k, v, beta, grow, scale_row, beta_row, tail, last, decay = ([] for _ in range(10))
        for i in each:
            raw_q = raw_ref[pl.ds(starts[i], CHUNK), 0:128]
            raw_k = raw_ref[pl.ds(starts[i], CHUNK), 128:256]
            raw_v = raw_ref[pl.ds(starts[i], CHUNK), 256:384]
            logits = raw_ref[pl.ds(starts[i], CHUNK), 384:512]
            q.append(
                (
                    raw_q
                    * lax.rsqrt(jnp.sum(raw_q * raw_q, -1, keepdims=True) + 1e-06)
                    * DK ** (-0.5)
                ).astype(bf16)
            )
            k.append(
                (raw_k * lax.rsqrt(jnp.sum(raw_k * raw_k, -1, keepdims=True) + 1e-06)).astype(bf16)
            )
            v.append(raw_v.astype(bf16))
            x = logits[:, 0:1]
            softplus = jnp.maximum(x, 0.0) + jnp.log1p(jnp.exp(-jnp.abs(x)))
            log_decay = (-rate * softplus).astype(bf16)
            strength = (1.0 / (1.0 + jnp.exp(-(logits[:, 1:2] + bias)))).astype(bf16).astype(f32)
            g = mm(ones_below, jnp.broadcast_to(log_decay, (CHUNK, CHUNK)))
            b = jnp.broadcast_to(strength, (CHUNK, CHUNK))
            turned = jnp.where(col < 64, g, b).T
            g_row, b_row = turned[0:1, :], turned[64:65, :]
            g_last = g_row[:, CHUNK - 1 : CHUNK]
            beta.append(b)
            grow.append(jnp.exp(g))
            beta_row.append(b_row)
            scale_row.append(b_row * jnp.exp(g_row))
            tail.append(jnp.exp(g_last - g))
            last.append(jnp.exp(g_last))
            decay.append(jnp.exp(jnp.where(inclusive, g - g_row, 0.0)))
        both = [mm(jnp.concatenate([q[i], k[i]], 0), k[i], 1, 1) for i in each]
        scores = [jnp.where(inclusive, both[i][:CHUNK] * decay[i], 0.0) for i in each]
        lower = [jnp.where(strict, beta[i] * decay[i] * both[i][CHUNK:], 0.0) for i in each]
        inverse = [eye - jnp.where(below(1), lower[i], 0.0) for i in each]
        for size in (2, 4, 8, 16, 32, 64):
            mask = below(size)
            inner = [mm(jnp.where(mask, lower[i], 0.0), inverse[i]) for i in each]
            inverse = [inverse[i] - mm(inverse[i], inner[i]) for i in each]
        rounded = [inverse[i].astype(bf16) for i in each]
        high = [lower[i].astype(bf16) for i in each]
        low = [(lower[i] - high[i].astype(f32)).astype(bf16) for i in each]
        rest = [
            eye - rounded[i].astype(f32) - mm(high[i], rounded[i]) - mm(low[i], rounded[i])
            for i in each
        ]
        inverse = [rounded[i].astype(f32) + mm(rounded[i], rest[i]) for i in each]
        w = [mm(inverse[i] * scale_row[i], k[i]) for i in each]
        u = [mm(inverse[i] * beta_row[i], v[i]) for i in each]
        wu = [jnp.concatenate([w[i], u[i]], 1) for i in each]
        tail2 = [jnp.concatenate([tail[i], tail[i]], 1) for i in each]
        change = [mm(wu[i] * tail2[i], k[i], 0, 0) for i in each]
        inside = [mm(scores[i], wu[i]) for i in each]
        reach = [grow[i] * q[i].astype(f32) - inside[i][:, :DK] for i in each]
        state, kept = state_ref[0 : DK + DV, :], state_ref[DK + DV :, :]
        for i in each:
            out = mm(reach[i], state, 1, 1)
            reach_ref[pl.ds(starts[i], CHUNK), :] = out[:, :DK].astype(bf16)
            own_ref[pl.ds(starts[i], CHUNK), :] = out[:, DK:] + inside[i][:, DK:]
            moved = mm(state, change[i][:DK])
            state = last[i] * state - moved
            state = jnp.concatenate([state[:DK], state[DK:] + change[i][DK:]], 0)
            kept = last[i] * kept
        state_ref[0 : DK + DV, :] = state
        state_ref[DK + DV :, :] = kept
        return carry

    lax.fori_loop(0, raw_ref.shape[0] // (CHUNK * GANG), gang, 0)

    @pl.when(pl.program_id(0) == pl.num_programs(0) - 1)
    def _():
        kept = state_ref[DK + DV :, :]
        part = kept.astype(bf16).astype(f32)
        total_ref[0:DK, :] = (state_ref[0:DK, :] - kept[0:1] * eye).astype(bf16)
        total_ref[DK : DK + DV, :] = state_ref[DK : DK + DV, :].astype(bf16)
        total_ref[DK + DV :, :] = jnp.concatenate([part, kept - part], 0).astype(bf16)


def opened(map_ref, *at):
    kept = map_ref[(*at, slice(DK + DV, MAP_ROWS))].astype(f32)
    change, shift = map_ref[(*at, slice(0, DK))], map_ref[(*at, slice(DK, DK + DV))]
    return change, shift.astype(f32), kept[0:1] + kept[8:9]


def join_kernel(core_ref, mine_ref, other_ref, copies_ref):
    def write(first_ref, second_ref):
        change, shift, kept = opened(first_ref)
        next_change, next_shift, next_kept = opened(second_ref)
        joined = kept * next_change.astype(f32) + next_kept * change.astype(f32)
        joined = (joined + mm(change, next_change)).astype(bf16)
        shift = (next_kept * shift + mm(shift, next_change) + next_shift).astype(bf16)
        kept = jnp.broadcast_to(kept * next_kept, (8, DK))
        part = kept.astype(bf16).astype(f32)
        kept = jnp.concatenate([part, kept - part], 0).astype(bf16)
        for i in range(copies_ref.shape[0]):
            copies_ref[i, 0:DK, :] = joined
            copies_ref[i, DK : DK + DV, :] = shift
            copies_ref[i, DK + DV : MAP_ROWS, :] = kept

    @pl.when(core_ref[0] == 0)
    def _():
        write(mine_ref, other_ref)

    @pl.when(core_ref[0] == 1)
    def _():
        write(other_ref, mine_ref)


def read_kernel(place_ref, map_ref, other_ref, reach_ref, own_ref, read_ref):
    def after(state, change, shift, kept):
        return kept * state + mm(state, change) + shift

    def one(j, state):
        return after(state, *opened(map_ref, j))

    state = lax.fori_loop(0, place_ref[0], one, jnp.zeros((DV, DK), f32))
    state = jnp.where(place_ref[1] == 1, after(state, *opened(other_ref)), state)
    read_ref[...] = (mm(reach_ref[...], state, 1, 1) + own_ref[...]).astype(bf16)


def shards(
    tokens, w_query, w_key, w_value, decay_proj, beta_proj, decay_rate, beta_bias, norm_gain
):
    local_rows = tokens.shape[0]
    streams = lax.axis_size("stream")
    head = lax.axis_index("stream")
    at_y, at_x, at_c = lax.axis_index("tm_0"), lax.axis_index("tm_1"), lax.axis_index("tm_2")
    vmem = pl.BlockSpec(memory_space=pltpu.VMEM)
    smem = pl.BlockSpec(memory_space=pltpu.SMEM)

    shares = 16
    rows = w_query.shape[0] // shares
    first = (at_y * 4 + at_x) * rows

    def share(w, width):
        return lax.dynamic_slice_in_dim(w, first, rows, 0).reshape(rows, HEADS, width)

    weights = jnp.concatenate(
        [
            share(w_query, DK),
            share(w_key, DK),
            share(w_value, DV),
            share(decay_proj, 1),
            share(beta_proj, 1),
            jnp.zeros((rows, HEADS, WIDE - 386), bf16),
        ],
        -1,
    ).transpose(1, 0, 2)
    all_tokens = lax.all_gather(tokens, "stream", axis=0, tiled=True)
    weights = lax.all_to_all(weights, "stream", split_axis=0, concat_axis=0, tiled=True)
    weights = jnp.broadcast_to(weights[None], (shares,) + weights.shape)
    weights = lax.all_to_all(weights, ("tm_0", "tm_1"), split_axis=0, concat_axis=0, tiled=True)
    weights = weights.transpose(1, 0, 2, 3).reshape(streams * shares * rows, WIDE)

    block_rows, features = all_tokens.shape
    stretch = CHUNK * GANG
    reach, own, total = pl.pallas_call(
        chunk_kernel,
        out_shape=(
            jax.ShapeDtypeStruct((block_rows, DK), bf16),
            jax.ShapeDtypeStruct((block_rows, DV), f32),
            jax.ShapeDtypeStruct((MAP_ROWS, DK), bf16),
        ),
        grid=(block_rows // stretch,),
        in_specs=[
            smem,
            smem,
            smem,
            pl.BlockSpec((stretch, features), lambda i: (i, 0)),
            pl.BlockSpec((features, WIDE), lambda i: (0, 0)),
        ],
        out_specs=(
            pl.BlockSpec((stretch, DK), lambda i: (i, 0)),
            pl.BlockSpec((stretch, DV), lambda i: (i, 0)),
            pl.BlockSpec((MAP_ROWS, DK), lambda i: (0, 0)),
        ),
        scratch_shapes=[
            pltpu.VMEM((stretch, WIDE), f32),
            pltpu.VMEM((DK + DV + 8, DK), f32),
        ],
        compiler_params=pltpu.CompilerParams(vmem_limit_bytes=48 * 2**20),
    )(head.reshape(1).astype(jnp.int32), decay_rate, beta_bias, all_tokens, weights)

    core = at_c.reshape(1).astype(jnp.int32)
    other = lax.ppermute(total, "tm_2", [(0, 1), (1, 0)])
    maps = pl.pallas_call(
        join_kernel,
        out_shape=jax.ShapeDtypeStruct((shares, MAP_ROWS, DK), bf16),
        in_specs=[smem, vmem, vmem],
        out_specs=vmem,
    )(core, total, other)
    maps = lax.all_to_all(maps, ("tm_0", "tm_1"), split_axis=0, concat_axis=0, tiled=True)
    place = jnp.stack([at_y * 4 + at_x, at_c]).astype(jnp.int32)
    readout = pl.pallas_call(
        read_kernel,
        out_shape=jax.ShapeDtypeStruct((block_rows, DV), bf16),
        in_specs=[smem, vmem, vmem, vmem, vmem],
        out_specs=vmem,
        compiler_params=pltpu.CompilerParams(vmem_limit_bytes=32 * 2**20),
    )(place, maps, other, reach, own)
    returned = lax.all_to_all(readout, "stream", split_axis=0, concat_axis=1, tiled=True)
    head_read = returned.reshape(local_rows, HEADS, DV).astype(f32)
    normed = (
        head_read
        * lax.rsqrt(jnp.mean(head_read * head_read, -1, keepdims=True) + 1e-06)
        * norm_gain
    )
    return normed.reshape(local_rows, HEADS * DV).astype(bf16)


def solution(mesh):
    finer = Mesh(
        mesh.devices.reshape(4, 4, 2, mesh.shape["stream"]), ("tm_0", "tm_1", "tm_2", "stream")
    )
    return jax.shard_map(
        shards,
        mesh=finer,
        in_specs=(
            P(TM_STREAM, None),
            P("stream", None),
            P("stream", None),
            P("stream", None),
            P("stream", None),
            P("stream", None),
            P(),
            P(),
            P(),
        ),
        out_specs=P(TM_STREAM, None),
        check_vma=False,
    )
```

```python
import jax
import jax.numpy as jnp
from jax import lax
from jax.experimental import pallas as pl
from jax.experimental.pallas import tpu as pltpu
from jax.sharding import Mesh
from jax.sharding import PartitionSpec as P

HEADS = 16
DK = 128
DV = 128
CHUNK = 128
GANG = 16
APART = 8
WIDE = 512
MAP_ROWS = 272
TM_STREAM = ("tm_0", "tm_1", "tm_2", "stream")
f32 = jnp.float32
bf16 = jnp.bfloat16


def mm(a, b, ca=1, cb=0):
    return lax.dot_general(
        a.astype(bf16), b.astype(bf16), (((ca,), (cb,)), ((), ())), preferred_element_type=f32
    )


def chunk_kernel(
    head_ref,
    rate_ref,
    bias_ref,
    token_ref,
    apart_ref,
    weight_ref,
    reach_ref,
    own_ref,
    total_ref,
    raw_ref,
    raw_apart_ref,
):
    step, steps = pl.program_id(0), pl.num_programs(0)
    rate, bias = rate_ref[head_ref[0]], bias_ref[head_ref[0]]
    for part_ref, part_raw_ref in ((token_ref, raw_ref), (apart_ref, raw_apart_ref)):
        size = part_ref.shape[0]
        part_raw_ref[pl.ds(pl.multiple_of(step * size, 8), size), :] = jnp.dot(
            part_ref[...], weight_ref[...], preferred_element_type=f32
        )

    @pl.when(step == steps - 1)
    def _():
        delta_rule(rate, bias, raw_ref, raw_apart_ref, reach_ref, own_ref, total_ref)


def delta_rule(rate, bias, raw_ref, raw_apart_ref, reach_ref, own_ref, total_ref):
    row = lax.broadcasted_iota(jnp.int32, (CHUNK, CHUNK), 0)
    col = lax.broadcasted_iota(jnp.int32, (CHUNK, CHUNK), 1)
    strict, inclusive = row > col, row >= col
    eye = jnp.where(row == col, 1.0, 0.0).astype(f32)
    ones_below = jnp.where(inclusive, 1.0, 0.0).astype(bf16)

    def below(size):
        return (
            (row // (2 * size) == col // (2 * size))
            & ((row // size) % 2 == 1)
            & ((col // size) % 2 == 0)
        )

    state = jnp.concatenate([eye, jnp.zeros((DV, DK), f32)], 0)
    kept = jnp.ones((8, DK), f32)
    most = CHUNK - APART
    for first in range(0, raw_ref.shape[0] // most, GANG):
        starts = [(first + i) * CHUNK for i in range(GANG)]
        each = range(GANG)
        q, k, v, beta, grow, scale_row, beta_row, tail, last, decay = ([] for _ in range(10))
        for i in each:
            raw = jnp.concatenate(
                [
                    raw_ref[pl.ds((first + i) * most, most), :],
                    raw_apart_ref[pl.ds((first + i) * APART, APART), :],
                ],
                0,
            )
            raw_q = raw[:, 0:128]
            raw_k = raw[:, 128:256]
            raw_v = raw[:, 256:384]
            logits = raw[:, 384:512]
            q.append(
                (
                    raw_q
                    * lax.rsqrt(jnp.sum(raw_q * raw_q, -1, keepdims=True) + 1e-06)
                    * DK ** (-0.5)
                ).astype(bf16)
            )
            k.append(
                (raw_k * lax.rsqrt(jnp.sum(raw_k * raw_k, -1, keepdims=True) + 1e-06)).astype(bf16)
            )
            v.append(raw_v.astype(bf16))
            x = logits[:, 0:1]
            softplus = jnp.maximum(x, 0.0) + jnp.log1p(jnp.exp(-jnp.abs(x)))
            log_decay = (-rate * softplus).astype(bf16)
            strength = (1.0 / (1.0 + jnp.exp(-(logits[:, 1:2] + bias)))).astype(bf16).astype(f32)
            g = mm(ones_below, jnp.broadcast_to(log_decay, (CHUNK, CHUNK)))
            b = jnp.broadcast_to(strength, (CHUNK, CHUNK))
            turned = jnp.where(col < 64, g, b).T
            g_row, b_row = turned[0:1, :], turned[64:65, :]
            g_last = g_row[:, CHUNK - 1 : CHUNK]
            beta.append(b)
            grow.append(jnp.exp(g))
            beta_row.append(b_row)
            scale_row.append(b_row * jnp.exp(g_row))
            tail.append(jnp.exp(g_last - g))
            last.append(jnp.exp(g_last))
            decay.append(jnp.exp(jnp.where(inclusive, g - g_row, 0.0)))
        both = [mm(jnp.concatenate([q[i], k[i]], 0), k[i], 1, 1) for i in each]
        scores = [jnp.where(inclusive, both[i][:CHUNK] * decay[i], 0.0) for i in each]
        lower = [jnp.where(strict, beta[i] * decay[i] * both[i][CHUNK:], 0.0) for i in each]
        inverse = [eye - jnp.where(below(1), lower[i], 0.0) for i in each]
        for size in (2, 4, 8, 16, 32, 64):
            mask = below(size)
            inner = [mm(jnp.where(mask, lower[i], 0.0), inverse[i]) for i in each]
            inverse = [inverse[i] - mm(inverse[i], inner[i]) for i in each]
        rounded = [inverse[i].astype(bf16) for i in each]
        high = [lower[i].astype(bf16) for i in each]
        rest = [eye - rounded[i].astype(f32) - mm(high[i], rounded[i]) for i in each]
        inverse = [rounded[i].astype(f32) + mm(rounded[i], rest[i]) for i in each]
        w = [mm(inverse[i] * scale_row[i], k[i]) for i in each]
        u = [mm(inverse[i] * beta_row[i], v[i]) for i in each]
        wu = [jnp.concatenate([w[i], u[i]], 1) for i in each]
        tail2 = [jnp.concatenate([tail[i], tail[i]], 1) for i in each]
        change = [mm(wu[i] * tail2[i], k[i], 0, 0) for i in each]
        inside = [mm(scores[i], wu[i]) for i in each]
        reach = [grow[i] * q[i].astype(f32) - inside[i][:, :DK] for i in each]
        for i in each:
            out = mm(reach[i], state, 1, 1)
            reach_ref[pl.ds(starts[i], CHUNK), :] = out[:, :DK].astype(bf16)
            own_ref[pl.ds(starts[i], CHUNK), :] = out[:, DK:] + inside[i][:, DK:]
            moved = mm(state, change[i][:DK])
            state = last[i] * state - moved
            state = jnp.concatenate([state[:DK], state[DK:] + change[i][DK:]], 0)
            kept = last[i] * kept
    part = kept.astype(bf16).astype(f32)
    total_ref[0:DK, :] = (state[:DK] - kept[0:1] * eye).astype(bf16)
    total_ref[DK : DK + DV, :] = state[DK:].astype(bf16)
    total_ref[DK + DV :, :] = jnp.concatenate([part, kept - part], 0).astype(bf16)


def opened(map_ref, *at):
    kept = map_ref[(*at, slice(DK + DV, MAP_ROWS))].astype(f32)
    change, shift = map_ref[(*at, slice(0, DK))], map_ref[(*at, slice(DK, DK + DV))]
    return change, shift.astype(f32), kept[0:1] + kept[8:9]


def join_kernel(core_ref, mine_ref, other_ref, copies_ref):
    def write(first_ref, second_ref):
        change, shift, kept = opened(first_ref)
        next_change, next_shift, next_kept = opened(second_ref)
        joined = kept * next_change.astype(f32) + next_kept * change.astype(f32)
        joined = (joined + mm(change, next_change)).astype(bf16)
        shift = (next_kept * shift + mm(shift, next_change) + next_shift).astype(bf16)
        kept = jnp.broadcast_to(kept * next_kept, (8, DK))
        part = kept.astype(bf16).astype(f32)
        kept = jnp.concatenate([part, kept - part], 0).astype(bf16)
        for i in range(copies_ref.shape[0]):
            copies_ref[i, 0:DK, :] = joined
            copies_ref[i, DK : DK + DV, :] = shift
            copies_ref[i, DK + DV : MAP_ROWS, :] = kept

    @pl.when(core_ref[0] == 0)
    def _():
        write(mine_ref, other_ref)

    @pl.when(core_ref[0] == 1)
    def _():
        write(other_ref, mine_ref)


def read_kernel(place_ref, map_ref, other_ref, reach_ref, own_ref, read_ref):
    def after(state, change, shift, kept):
        return kept * state + mm(state, change) + shift

    def one(j, state):
        return after(state, *opened(map_ref, j))

    state = lax.fori_loop(0, place_ref[0], one, jnp.zeros((DV, DK), f32))
    state = jnp.where(place_ref[1] == 1, after(state, *opened(other_ref)), state)
    read_ref[...] = (mm(reach_ref[...], state, 1, 1) + own_ref[...]).astype(bf16)


def shards(
    tokens, w_query, w_key, w_value, decay_proj, beta_proj, decay_rate, beta_bias, norm_gain
):
    local_rows = tokens.shape[0]
    streams = lax.axis_size("stream")
    head = lax.axis_index("stream")
    at_y, at_x, at_c = lax.axis_index("tm_0"), lax.axis_index("tm_1"), lax.axis_index("tm_2")
    vmem = pl.BlockSpec(memory_space=pltpu.VMEM)
    smem = pl.BlockSpec(memory_space=pltpu.SMEM)

    shares = 16
    rows = w_query.shape[0] // shares
    first = (at_y * 4 + at_x) * rows

    def share(w, width):
        return lax.dynamic_slice_in_dim(w, first, rows, 0).reshape(rows, HEADS, width)

    weights = jnp.concatenate(
        [
            share(w_query, DK),
            share(w_key, DK),
            share(w_value, DV),
            share(decay_proj, 1),
            share(beta_proj, 1),
            jnp.zeros((rows, HEADS, WIDE - 386), bf16),
        ],
        -1,
    ).transpose(1, 0, 2)
    most = local_rows - APART
    all_tokens = lax.all_gather(tokens[:most], "stream", axis=0, tiled=True)
    apart = lax.all_gather(tokens[most:], "stream", axis=0, tiled=True)
    weights = lax.all_to_all(weights, "stream", split_axis=0, concat_axis=0, tiled=True)
    weights = jnp.broadcast_to(weights[None], (shares,) + weights.shape)
    weights = lax.all_to_all(weights, ("tm_0", "tm_1"), split_axis=0, concat_axis=0, tiled=True)
    weights = weights.transpose(1, 0, 2, 3).reshape(streams * shares * rows, WIDE)

    features = all_tokens.shape[1]
    block_rows = streams * local_rows
    steps = 2
    reach, own, total = pl.pallas_call(
        chunk_kernel,
        out_shape=(
            jax.ShapeDtypeStruct((block_rows, DK), bf16),
            jax.ShapeDtypeStruct((block_rows, DV), f32),
            jax.ShapeDtypeStruct((MAP_ROWS, DK), bf16),
        ),
        grid=(steps,),
        in_specs=[
            smem,
            smem,
            smem,
            pl.BlockSpec((streams * most // steps, features), lambda i: (i, 0)),
            pl.BlockSpec((streams * APART // steps, features), lambda i: (i, 0)),
            pl.BlockSpec((features, WIDE), lambda i: (0, 0)),
        ],
        out_specs=(
            pl.BlockSpec((block_rows, DK), lambda i: (0, 0)),
            pl.BlockSpec((block_rows, DV), lambda i: (0, 0)),
            pl.BlockSpec((MAP_ROWS, DK), lambda i: (0, 0)),
        ),
        scratch_shapes=[
            pltpu.VMEM((streams * most, WIDE), f32),
            pltpu.VMEM((streams * APART, WIDE), f32),
        ],
        compiler_params=pltpu.CompilerParams(vmem_limit_bytes=48 * 2**20),
    )(head.reshape(1).astype(jnp.int32), decay_rate, beta_bias, all_tokens, apart, weights)

    core = at_c.reshape(1).astype(jnp.int32)
    other = lax.ppermute(total, "tm_2", [(0, 1), (1, 0)])
    maps = pl.pallas_call(
        join_kernel,
        out_shape=jax.ShapeDtypeStruct((shares, MAP_ROWS, DK), bf16),
        in_specs=[smem, vmem, vmem],
        out_specs=vmem,
    )(core, total, other)
    maps = lax.all_to_all(maps, ("tm_0", "tm_1"), split_axis=0, concat_axis=0, tiled=True)
    place = jnp.stack([at_y * 4 + at_x, at_c]).astype(jnp.int32)
    readout = pl.pallas_call(
        read_kernel,
        out_shape=jax.ShapeDtypeStruct((block_rows, DV), bf16),
        in_specs=[smem, vmem, vmem, vmem, vmem],
        out_specs=vmem,
        compiler_params=pltpu.CompilerParams(vmem_limit_bytes=32 * 2**20),
    )(place, maps, other, reach, own)
    returned = lax.all_to_all(readout, "stream", split_axis=0, concat_axis=1, tiled=True)
    head_read = returned.reshape(local_rows, HEADS, DV).astype(f32)
    normed = (
        head_read
        * lax.rsqrt(jnp.mean(head_read * head_read, -1, keepdims=True) + 1e-06)
        * norm_gain
    )
    return normed.reshape(local_rows, HEADS * DV).astype(bf16)


def solution(mesh):
    finer = Mesh(
        mesh.devices.reshape(4, 4, 2, mesh.shape["stream"]), ("tm_0", "tm_1", "tm_2", "stream")
    )
    return jax.shard_map(
        shards,
        mesh=finer,
        in_specs=(
            P(TM_STREAM, None),
            P("stream", None),
            P("stream", None),
            P("stream", None),
            P("stream", None),
            P("stream", None),
            P(),
            P(),
            P(),
        ),
        out_specs=P(TM_STREAM, None),
        check_vma=False,
    )
```

```python
import jax
import jax.numpy as jnp
from jax import lax
from jax.experimental import pallas as pl
from jax.experimental.pallas import tpu as pltpu
from jax.sharding import Mesh
from jax.sharding import PartitionSpec as P

HEADS = 16
DK = 128
DV = 128
CHUNK = 128
GANG = 16
WIDE = 512
MAP_ROWS = 272
TM_STREAM = ("tm_0", "tm_1", "tm_2", "stream")
f32 = jnp.float32
bf16 = jnp.bfloat16


def mm(a, b, ca=1, cb=0):
    return lax.dot_general(
        a.astype(bf16), b.astype(bf16), (((ca,), (cb,)), ((), ())), preferred_element_type=f32
    )


def chunk_kernel(
    head_ref,
    rate_ref,
    bias_ref,
    token_ref,
    mine_ref,
    other_ref,
    reach_ref,
    own_ref,
    total_ref,
    raw_ref,
):
    step, steps = pl.program_id(0), pl.num_programs(0)
    rate, bias = rate_ref[head_ref[0]], bias_ref[head_ref[0]]
    size = token_ref.shape[0]
    rows = pl.ds(pl.multiple_of(step * size, size), size)
    half = mine_ref.shape[1]
    for c in range(2):
        weights = jnp.where(head_ref[1] == c, mine_ref[...], other_ref[...])
        raw_ref[rows, c * half : (c + 1) * half] = jnp.dot(
            token_ref[...], weights, preferred_element_type=f32
        )

    @pl.when(step == steps - 1)
    def _():
        delta_rule(rate, bias, raw_ref, reach_ref, own_ref, total_ref)


def delta_rule(rate, bias, raw_ref, reach_ref, own_ref, total_ref):
    row = lax.broadcasted_iota(jnp.int32, (CHUNK, CHUNK), 0)
    col = lax.broadcasted_iota(jnp.int32, (CHUNK, CHUNK), 1)
    strict, inclusive = row > col, row >= col
    eye = jnp.where(row == col, 1.0, 0.0).astype(f32)
    ones_below = jnp.where(inclusive, 1.0, 0.0).astype(bf16)

    def below(size):
        return (
            (row // (2 * size) == col // (2 * size))
            & ((row // size) % 2 == 1)
            & ((col // size) % 2 == 0)
        )

    state = jnp.concatenate([eye, jnp.zeros((DV, DK), f32)], 0)
    kept = jnp.ones((8, DK), f32)
    for first in range(0, raw_ref.shape[0] // CHUNK, GANG):
        starts = [(first + i) * CHUNK for i in range(GANG)]
        each = range(GANG)
        q, k, v, beta, grow, scale_row, beta_row, tail, last, decay = ([] for _ in range(10))
        for i in each:
            raw = raw_ref[pl.ds(starts[i], CHUNK), :]
            raw_q = raw[:, 0:128]
            raw_k = raw[:, 128:256]
            raw_v = raw[:, 256:384]
            logits = raw[:, 384:512]
            q.append(
                (
                    raw_q
                    * lax.rsqrt(jnp.sum(raw_q * raw_q, -1, keepdims=True) + 1e-06)
                    * DK ** (-0.5)
                ).astype(bf16)
            )
            k.append(
                (raw_k * lax.rsqrt(jnp.sum(raw_k * raw_k, -1, keepdims=True) + 1e-06)).astype(bf16)
            )
            v.append(raw_v.astype(bf16))
            x = logits[:, 0:1]
            softplus = jnp.maximum(x, 0.0) + jnp.log1p(jnp.exp(-jnp.abs(x)))
            log_decay = (-rate * softplus).astype(bf16)
            strength = (1.0 / (1.0 + jnp.exp(-(logits[:, 1:2] + bias)))).astype(bf16).astype(f32)
            g = mm(ones_below, jnp.broadcast_to(log_decay, (CHUNK, CHUNK)))
            b = jnp.broadcast_to(strength, (CHUNK, CHUNK))
            turned = jnp.where(col < 64, g, b).T
            g_row, b_row = turned[0:1, :], turned[64:65, :]
            g_last = g_row[:, CHUNK - 1 : CHUNK]
            beta.append(b)
            grow.append(jnp.exp(g))
            beta_row.append(b_row)
            scale_row.append(b_row * jnp.exp(g_row))
            tail.append(jnp.exp(g_last - g))
            last.append(jnp.exp(g_last))
            decay.append(jnp.exp(jnp.where(inclusive, g - g_row, 0.0)))
        both = [mm(jnp.concatenate([q[i], k[i]], 0), k[i], 1, 1) for i in each]
        scores = [jnp.where(inclusive, both[i][:CHUNK] * decay[i], 0.0) for i in each]
        lower = [jnp.where(strict, beta[i] * decay[i] * both[i][CHUNK:], 0.0) for i in each]
        inverse = [eye - jnp.where(below(1), lower[i], 0.0) for i in each]
        for size in (2, 4, 8, 16, 32, 64):
            mask = below(size)
            inner = [mm(jnp.where(mask, lower[i], 0.0), inverse[i]) for i in each]
            inverse = [inverse[i] - mm(inverse[i], inner[i]) for i in each]
        rounded = [inverse[i].astype(bf16) for i in each]
        high = [lower[i].astype(bf16) for i in each]
        rest = [eye - rounded[i].astype(f32) - mm(high[i], rounded[i]) for i in each]
        inverse = [rounded[i].astype(f32) + mm(rounded[i], rest[i]) for i in each]
        w = [mm(inverse[i] * scale_row[i], k[i]) for i in each]
        u = [mm(inverse[i] * beta_row[i], v[i]) for i in each]
        wu = [jnp.concatenate([w[i], u[i]], 1) for i in each]
        tail2 = [jnp.concatenate([tail[i], tail[i]], 1) for i in each]
        change = [mm(wu[i] * tail2[i], k[i], 0, 0) for i in each]
        inside = [mm(scores[i], wu[i]) for i in each]
        reach = [grow[i] * q[i].astype(f32) - inside[i][:, :DK] for i in each]
        for i in each:
            out = mm(reach[i], state, 1, 1)
            reach_ref[pl.ds(starts[i], CHUNK), :] = out[:, :DK].astype(bf16)
            own_ref[pl.ds(starts[i], CHUNK), :] = out[:, DK:] + inside[i][:, DK:]
            moved = mm(state, change[i][:DK])
            state = last[i] * state - moved
            state = jnp.concatenate([state[:DK], state[DK:] + change[i][DK:]], 0)
            kept = last[i] * kept
    part = kept.astype(bf16).astype(f32)
    total_ref[0:DK, :] = (state[:DK] - kept[0:1] * eye).astype(bf16)
    total_ref[DK : DK + DV, :] = state[DK:].astype(bf16)
    total_ref[DK + DV :, :] = jnp.concatenate([part, kept - part], 0).astype(bf16)


def opened(map_ref, *at):
    kept = map_ref[(*at, slice(DK + DV, MAP_ROWS))].astype(f32)
    change, shift = map_ref[(*at, slice(0, DK))], map_ref[(*at, slice(DK, DK + DV))]
    return change, shift.astype(f32), kept[0:1] + kept[8:9]


def join_kernel(core_ref, mine_ref, other_ref, copies_ref):
    def write(first_ref, second_ref):
        change, shift, kept = opened(first_ref)
        next_change, next_shift, next_kept = opened(second_ref)
        joined = kept * next_change.astype(f32) + next_kept * change.astype(f32)
        joined = (joined + mm(change, next_change)).astype(bf16)
        shift = (next_kept * shift + mm(shift, next_change) + next_shift).astype(bf16)
        kept = jnp.broadcast_to(kept * next_kept, (8, DK))
        part = kept.astype(bf16).astype(f32)
        kept = jnp.concatenate([part, kept - part], 0).astype(bf16)
        for i in range(copies_ref.shape[0]):
            copies_ref[i, 0:DK, :] = joined
            copies_ref[i, DK : DK + DV, :] = shift
            copies_ref[i, DK + DV : MAP_ROWS, :] = kept

    @pl.when(core_ref[0] == 0)
    def _():
        write(mine_ref, other_ref)

    @pl.when(core_ref[0] == 1)
    def _():
        write(other_ref, mine_ref)


def read_kernel(place_ref, map_ref, other_ref, reach_ref, own_ref, read_ref):
    def after(state, change, shift, kept):
        return kept * state + mm(state, change) + shift

    def one(j, state):
        return after(state, *opened(map_ref, j))

    state = lax.fori_loop(0, place_ref[0], one, jnp.zeros((DV, DK), f32))
    state = jnp.where(place_ref[1] == 1, after(state, *opened(other_ref)), state)
    read_ref[...] = (mm(reach_ref[...], state, 1, 1) + own_ref[...]).astype(bf16)


def shards(
    tokens, w_query, w_key, w_value, decay_proj, beta_proj, decay_rate, beta_bias, norm_gain
):
    local_rows = tokens.shape[0]
    streams = lax.axis_size("stream")
    head = lax.axis_index("stream")
    at_y, at_x, at_c = lax.axis_index("tm_0"), lax.axis_index("tm_1"), lax.axis_index("tm_2")
    vmem = pl.BlockSpec(memory_space=pltpu.VMEM)
    smem = pl.BlockSpec(memory_space=pltpu.SMEM)

    shares = 16
    rows = w_query.shape[0] // shares
    first = (at_y * 4 + at_x) * rows

    def share(w, width):
        return lax.dynamic_slice_in_dim(w, first, rows, 0).reshape(rows, HEADS, width)

    pads = jnp.zeros((rows, HEADS, WIDE - 386), bf16)
    left = jnp.concatenate([share(w_query, DK), share(w_key, DK)], -1)
    right = jnp.concatenate(
        [share(w_value, DV), share(decay_proj, 1), share(beta_proj, 1), pads], -1
    )
    weights = jnp.where(at_c == 0, left, right).transpose(1, 0, 2)
    all_tokens = lax.all_gather(tokens, "stream", axis=0, tiled=True)
    weights = lax.all_to_all(weights, "stream", split_axis=0, concat_axis=0, tiled=True)
    weights = jnp.broadcast_to(weights[None], (shares,) + weights.shape)
    weights = lax.all_to_all(weights, ("tm_0", "tm_1"), split_axis=0, concat_axis=0, tiled=True)
    weights = weights.transpose(1, 0, 2, 3).reshape(streams * shares * rows, WIDE // 2)
    swapped = lax.ppermute(weights, "tm_2", [(0, 1), (1, 0)])

    block_rows, features = all_tokens.shape
    steps = 2
    reach, own, total = pl.pallas_call(
        chunk_kernel,
        out_shape=(
            jax.ShapeDtypeStruct((block_rows, DK), bf16),
            jax.ShapeDtypeStruct((block_rows, DV), f32),
            jax.ShapeDtypeStruct((MAP_ROWS, DK), bf16),
        ),
        grid=(steps,),
        in_specs=[
            smem,
            smem,
            smem,
            pl.BlockSpec((block_rows // steps, features), lambda i: (i, 0)),
            pl.BlockSpec((features, WIDE // 2), lambda i: (0, 0)),
            pl.BlockSpec((features, WIDE // 2), lambda i: (0, 0)),
        ],
        out_specs=(
            pl.BlockSpec((block_rows, DK), lambda i: (0, 0)),
            pl.BlockSpec((block_rows, DV), lambda i: (0, 0)),
            pl.BlockSpec((MAP_ROWS, DK), lambda i: (0, 0)),
        ),
        scratch_shapes=[
            pltpu.VMEM((block_rows, WIDE), f32),
        ],
        compiler_params=pltpu.CompilerParams(vmem_limit_bytes=48 * 2**20),
    )(
        jnp.stack([head, at_c]).astype(jnp.int32),
        decay_rate,
        beta_bias,
        all_tokens,
        weights,
        swapped,
    )

    core = at_c.reshape(1).astype(jnp.int32)
    other = lax.ppermute(total, "tm_2", [(0, 1), (1, 0)])
    maps = pl.pallas_call(
        join_kernel,
        out_shape=jax.ShapeDtypeStruct((shares, MAP_ROWS, DK), bf16),
        in_specs=[smem, vmem, vmem],
        out_specs=vmem,
    )(core, total, other)
    maps = lax.all_to_all(maps, ("tm_0", "tm_1"), split_axis=0, concat_axis=0, tiled=True)
    place = jnp.stack([at_y * 4 + at_x, at_c]).astype(jnp.int32)
    readout = pl.pallas_call(
        read_kernel,
        out_shape=jax.ShapeDtypeStruct((block_rows, DV), bf16),
        in_specs=[smem, vmem, vmem, vmem, vmem],
        out_specs=vmem,
        compiler_params=pltpu.CompilerParams(vmem_limit_bytes=32 * 2**20),
    )(place, maps, other, reach, own)
    returned = lax.all_to_all(readout, "stream", split_axis=0, concat_axis=1, tiled=True)
    head_read = returned.reshape(local_rows, HEADS, DV).astype(f32)
    normed = (
        head_read
        * lax.rsqrt(jnp.mean(head_read * head_read, -1, keepdims=True) + 1e-06)
        * norm_gain
    )
    return normed.reshape(local_rows, HEADS * DV).astype(bf16)


def solution(mesh):
    finer = Mesh(
        mesh.devices.reshape(4, 4, 2, mesh.shape["stream"]), ("tm_0", "tm_1", "tm_2", "stream")
    )
    return jax.shard_map(
        shards,
        mesh=finer,
        in_specs=(
            P(TM_STREAM, None),
            P("stream", None),
            P("stream", None),
            P("stream", None),
            P("stream", None),
            P("stream", None),
            P(),
            P(),
            P(),
        ),
        out_specs=P(TM_STREAM, None),
        check_vma=False,
    )
```

```python
import jax
import jax.numpy as jnp
from jax import lax
from jax.experimental import pallas as pl
from jax.experimental.pallas import tpu as pltpu
from jax.sharding import Mesh
from jax.sharding import PartitionSpec as P

HEADS = 16
DK = 128
DV = 128
CHUNK = 128
GANG = 16
WIDE = 512
MAP_ROWS = 272
TM_STREAM = ("tm_0", "tm_1", "tm_2", "stream")
f32 = jnp.float32
bf16 = jnp.bfloat16


def mm(a, b, ca=1, cb=0):
    return lax.dot_general(
        a.astype(bf16), b.astype(bf16), (((ca,), (cb,)), ((), ())), preferred_element_type=f32
    )


def chunk_kernel(
    head_ref,
    rate_ref,
    bias_ref,
    token_ref,
    mine_ref,
    other_ref,
    total_ref,
    query_ref,
    key_ref,
    level_ref,
    solved_ref,
    state_ref,
    raw_ref,
):
    step, steps = pl.program_id(0), pl.num_programs(0)
    rate, bias = rate_ref[head_ref[0]], bias_ref[head_ref[0]]
    size = token_ref.shape[0]
    rows = pl.ds(pl.multiple_of(step * size, size), size)
    half = mine_ref.shape[1]
    for c in range(2):
        weights = jnp.where(head_ref[1] == c, mine_ref[...], other_ref[...])
        raw_ref[rows, c * half : (c + 1) * half] = jnp.dot(
            token_ref[...], weights, preferred_element_type=f32
        )

    @pl.when(step == steps - 1)
    def _():
        for start in range(0, raw_ref.shape[0], CHUNK):
            query_ref[start : start + CHUNK, :] = raw_ref[start : start + CHUNK, 0:128]
        run_map(rate, bias, raw_ref, total_ref, key_ref, level_ref, solved_ref, state_ref)


def run_map(rate, bias, raw_ref, total_ref, key_ref, level_ref, solved_ref, state_ref):
    row = lax.broadcasted_iota(jnp.int32, (CHUNK, CHUNK), 0)
    col = lax.broadcasted_iota(jnp.int32, (CHUNK, CHUNK), 1)
    strict, inclusive = row > col, row >= col
    eye = jnp.where(row == col, 1.0, 0.0).astype(f32)
    ones_below = jnp.where(inclusive, 1.0, 0.0).astype(bf16)

    def below(size):
        return (
            (row // (2 * size) == col // (2 * size))
            & ((row // size) % 2 == 1)
            & ((col // size) % 2 == 0)
        )

    state = jnp.concatenate([eye, jnp.zeros((DV, DK), f32)], 0)
    kept = jnp.ones((8, DK), f32)
    for first in range(0, raw_ref.shape[0] // CHUNK, GANG):
        starts = [(first + i) * CHUNK for i in range(GANG)]
        each = range(GANG)
        k, v, beta, scale_row, beta_row, tail, last, decay = ([] for _ in range(8))
        for i in each:
            raw = raw_ref[pl.ds(starts[i], CHUNK), :]
            raw_k = raw[:, 128:256]
            raw_v = raw[:, 256:384]
            logits = raw[:, 384:512]
            k.append(
                (raw_k * lax.rsqrt(jnp.sum(raw_k * raw_k, -1, keepdims=True) + 1e-06)).astype(bf16)
            )
            v.append(raw_v.astype(bf16))
            key_ref[pl.ds(starts[i], CHUNK), :] = k[i]
            x = logits[:, 0:1]
            softplus = jnp.maximum(x, 0.0) + jnp.log1p(jnp.exp(-jnp.abs(x)))
            log_decay = (-rate * softplus).astype(bf16)
            strength = (1.0 / (1.0 + jnp.exp(-(logits[:, 1:2] + bias)))).astype(bf16).astype(f32)
            g = mm(ones_below, jnp.broadcast_to(log_decay, (CHUNK, CHUNK)))
            b = jnp.broadcast_to(strength, (CHUNK, CHUNK))
            turned = jnp.where(col < 64, g, b).T
            g_row, b_row = turned[0:1, :], turned[64:65, :]
            g_last = g_row[:, CHUNK - 1 : CHUNK]
            beta.append(b)
            level_ref[pl.ds(starts[i], CHUNK), :] = g
            beta_row.append(b_row)
            scale_row.append(b_row * jnp.exp(g_row))
            tail.append(jnp.exp(g_last - g))
            last.append(jnp.exp(g_last))
            decay.append(jnp.exp(jnp.where(inclusive, g - g_row, 0.0)))
        products = [mm(k[i], k[i], 1, 1) for i in each]
        lower = [jnp.where(strict, beta[i] * decay[i] * products[i], 0.0) for i in each]
        inverse = [eye - jnp.where(below(1), lower[i], 0.0) for i in each]
        for size in (2, 4, 8, 16, 32, 64):
            mask = below(size)
            inner = [mm(jnp.where(mask, lower[i], 0.0), inverse[i]) for i in each]
            inverse = [inverse[i] - mm(inverse[i], inner[i]) for i in each]
        rounded = [inverse[i].astype(bf16) for i in each]
        high = [lower[i].astype(bf16) for i in each]
        rest = [eye - rounded[i].astype(f32) - mm(high[i], rounded[i]) for i in each]
        inverse = [rounded[i].astype(f32) + mm(rounded[i], rest[i]) for i in each]
        w = [mm(inverse[i] * scale_row[i], k[i]) for i in each]
        u = [mm(inverse[i] * beta_row[i], v[i]) for i in each]
        wu = [jnp.concatenate([w[i], u[i]], 1) for i in each]
        tail2 = [jnp.concatenate([tail[i], tail[i]], 1) for i in each]
        change = [mm(wu[i] * tail2[i], k[i], 0, 0) for i in each]
        for i in each:
            solved_ref[pl.ds(starts[i], CHUNK), :] = wu[i].astype(bf16)
            state_ref[first + i] = state.astype(bf16)
            moved = mm(state, change[i][:DK])
            state = last[i] * state - moved
            state = jnp.concatenate([state[:DK], state[DK:] + change[i][DK:]], 0)
            kept = last[i] * kept
    part = kept.astype(bf16).astype(f32)
    total_ref[0:DK, :] = (state[:DK] - kept[0:1] * eye).astype(bf16)
    total_ref[DK : DK + DV, :] = state[DK:].astype(bf16)
    total_ref[DK + DV :, :] = jnp.concatenate([part, kept - part], 0).astype(bf16)


def reach_kernel(query_ref, key_ref, level_ref, solved_ref, state_ref, reach_ref, own_ref):
    row = lax.broadcasted_iota(jnp.int32, (CHUNK, CHUNK), 0)
    col = lax.broadcasted_iota(jnp.int32, (CHUNK, CHUNK), 1)
    inclusive = row >= col

    gang = 8

    def some(step, carry):
        each = range(gang)
        spans = [pl.ds(pl.multiple_of((step * gang + i) * CHUNK, CHUNK), CHUNK) for i in each]
        q, scores, reach = [], [], []
        for i in each:
            raw_q = query_ref[spans[i], :]
            scale = lax.rsqrt(jnp.sum(raw_q * raw_q, -1, keepdims=True) + 1e-06)
            q.append((raw_q * scale * DK ** (-0.5)).astype(bf16))
        products = [mm(q[i], key_ref[spans[i], :], 1, 1) for i in each]
        for i in each:
            g = level_ref[spans[i], :]
            decay = jnp.exp(jnp.where(inclusive, g - g.T, 0.0))
            scores.append(jnp.where(inclusive, products[i] * decay, 0.0))
        inside = [mm(scores[i], solved_ref[spans[i], :]) for i in each]
        for i in each:
            grown = jnp.exp(level_ref[spans[i], :]) * q[i].astype(f32)
            reach.append(grown - inside[i][:, :DK])
        out = [mm(reach[i], state_ref[step * gang + i], 1, 1) for i in each]
        for i in each:
            reach_ref[spans[i], :] = out[i][:, :DK].astype(bf16)
            own_ref[spans[i], :] = out[i][:, DK:] + inside[i][:, DK:]
        return carry

    lax.fori_loop(0, state_ref.shape[0] // gang, some, 0)


def opened(map_ref, *at):
    kept = map_ref[(*at, slice(DK + DV, MAP_ROWS))].astype(f32)
    change, shift = map_ref[(*at, slice(0, DK))], map_ref[(*at, slice(DK, DK + DV))]
    return change, shift.astype(f32), kept[0:1] + kept[8:9]


def join_kernel(core_ref, mine_ref, other_ref, copies_ref):
    def write(first_ref, second_ref):
        change, shift, kept = opened(first_ref)
        next_change, next_shift, next_kept = opened(second_ref)
        joined = kept * next_change.astype(f32) + next_kept * change.astype(f32)
        joined = (joined + mm(change, next_change)).astype(bf16)
        shift = (next_kept * shift + mm(shift, next_change) + next_shift).astype(bf16)
        kept = jnp.broadcast_to(kept * next_kept, (8, DK))
        part = kept.astype(bf16).astype(f32)
        kept = jnp.concatenate([part, kept - part], 0).astype(bf16)
        for i in range(copies_ref.shape[0]):
            copies_ref[i, 0:DK, :] = joined
            copies_ref[i, DK : DK + DV, :] = shift
            copies_ref[i, DK + DV : MAP_ROWS, :] = kept

    @pl.when(core_ref[0] == 0)
    def _():
        write(mine_ref, other_ref)

    @pl.when(core_ref[0] == 1)
    def _():
        write(other_ref, mine_ref)


def read_kernel(place_ref, map_ref, other_ref, reach_ref, own_ref, read_ref):
    def after(state, change, shift, kept):
        return kept * state + mm(state, change) + shift

    def one(j, state):
        return after(state, *opened(map_ref, j))

    state = lax.fori_loop(0, place_ref[0], one, jnp.zeros((DV, DK), f32))
    state = jnp.where(place_ref[1] == 1, after(state, *opened(other_ref)), state)
    read_ref[...] = (mm(reach_ref[...], state, 1, 1) + own_ref[...]).astype(bf16)


def shards(
    tokens, w_query, w_key, w_value, decay_proj, beta_proj, decay_rate, beta_bias, norm_gain
):
    local_rows = tokens.shape[0]
    streams = lax.axis_size("stream")
    head = lax.axis_index("stream")
    at_y, at_x, at_c = lax.axis_index("tm_0"), lax.axis_index("tm_1"), lax.axis_index("tm_2")
    vmem = pl.BlockSpec(memory_space=pltpu.VMEM)
    smem = pl.BlockSpec(memory_space=pltpu.SMEM)

    shares = 16
    rows = w_query.shape[0] // shares
    first = (at_y * 4 + at_x) * rows

    def share(w, width):
        return lax.dynamic_slice_in_dim(w, first, rows, 0).reshape(rows, HEADS, width)

    pads = jnp.zeros((rows, HEADS, WIDE - 386), bf16)
    left = jnp.concatenate([share(w_query, DK), share(w_key, DK)], -1)
    right = jnp.concatenate(
        [share(w_value, DV), share(decay_proj, 1), share(beta_proj, 1), pads], -1
    )
    weights = jnp.where(at_c == 0, left, right).transpose(1, 0, 2)
    all_tokens = lax.all_gather(tokens, "stream", axis=0, tiled=True)
    weights = lax.all_to_all(weights, "stream", split_axis=0, concat_axis=0, tiled=True)
    weights = jnp.broadcast_to(weights[None], (shares,) + weights.shape)
    weights = lax.all_to_all(weights, ("tm_0", "tm_1"), split_axis=0, concat_axis=0, tiled=True)
    weights = weights.transpose(1, 0, 2, 3).reshape(streams * shares * rows, WIDE // 2)
    swapped = lax.ppermute(weights, "tm_2", [(0, 1), (1, 0)])

    block_rows, features = all_tokens.shape
    steps = 2
    total, *kept = pl.pallas_call(
        chunk_kernel,
        out_shape=(
            jax.ShapeDtypeStruct((MAP_ROWS, DK), bf16),
            jax.ShapeDtypeStruct((block_rows, DK), f32),
            jax.ShapeDtypeStruct((block_rows, DK), bf16),
            jax.ShapeDtypeStruct((block_rows, CHUNK), f32),
            jax.ShapeDtypeStruct((block_rows, DK + DV), bf16),
            jax.ShapeDtypeStruct((block_rows // CHUNK, DK + DV, DK), bf16),
        ),
        grid=(steps,),
        in_specs=[
            smem,
            smem,
            smem,
            pl.BlockSpec((block_rows // steps, features), lambda i: (i, 0)),
            pl.BlockSpec((features, WIDE // 2), lambda i: (0, 0)),
            pl.BlockSpec((features, WIDE // 2), lambda i: (0, 0)),
        ],
        out_specs=(
            pl.BlockSpec((MAP_ROWS, DK), lambda i: (0, 0)),
            pl.BlockSpec((block_rows, DK), lambda i: (0, 0)),
            pl.BlockSpec((block_rows, DK), lambda i: (0, 0)),
            pl.BlockSpec((block_rows, CHUNK), lambda i: (0, 0)),
            pl.BlockSpec((block_rows, DK + DV), lambda i: (0, 0)),
            pl.BlockSpec((block_rows // CHUNK, DK + DV, DK), lambda i: (0, 0, 0)),
        ),
        scratch_shapes=[
            pltpu.VMEM((block_rows, WIDE), f32),
        ],
        compiler_params=pltpu.CompilerParams(vmem_limit_bytes=36 * 2**20),
    )(
        jnp.stack([head, at_c]).astype(jnp.int32),
        decay_rate,
        beta_bias,
        all_tokens,
        weights,
        swapped,
    )

    reach, own = pl.pallas_call(
        reach_kernel,
        out_shape=(
            jax.ShapeDtypeStruct((block_rows, DK), bf16),
            jax.ShapeDtypeStruct((block_rows, DV), f32),
        ),
        in_specs=[vmem] * 5,
        out_specs=(vmem, vmem),
        compiler_params=pltpu.CompilerParams(vmem_limit_bytes=20 * 2**20),
        cost_estimate=pl.CostEstimate(
            flops=10 * block_rows * CHUNK * DK, bytes_accessed=6 * 2**20, transcendentals=0
        ),
    )(*kept)
    core = at_c.reshape(1).astype(jnp.int32)
    other = lax.ppermute(total, "tm_2", [(0, 1), (1, 0)])
    maps = pl.pallas_call(
        join_kernel,
        out_shape=jax.ShapeDtypeStruct((shares, MAP_ROWS, DK), bf16),
        in_specs=[smem, vmem, vmem],
        out_specs=vmem,
    )(core, total, other)
    maps = lax.all_to_all(maps, ("tm_0", "tm_1"), split_axis=0, concat_axis=0, tiled=True)
    place = jnp.stack([at_y * 4 + at_x, at_c]).astype(jnp.int32)
    readout = pl.pallas_call(
        read_kernel,
        out_shape=jax.ShapeDtypeStruct((block_rows, DV), bf16),
        in_specs=[smem, vmem, vmem, vmem, vmem],
        out_specs=vmem,
        compiler_params=pltpu.CompilerParams(vmem_limit_bytes=12 * 2**20),
    )(place, maps, other, reach, own)
    returned = lax.all_to_all(readout, "stream", split_axis=0, concat_axis=1, tiled=True)
    head_read = returned.reshape(local_rows, HEADS, DV).astype(f32)
    normed = (
        head_read
        * lax.rsqrt(jnp.mean(head_read * head_read, -1, keepdims=True) + 1e-06)
        * norm_gain
    )
    return normed.reshape(local_rows, HEADS * DV).astype(bf16)


def solution(mesh):
    finer = Mesh(
        mesh.devices.reshape(4, 4, 2, mesh.shape["stream"]), ("tm_0", "tm_1", "tm_2", "stream")
    )
    return jax.shard_map(
        shards,
        mesh=finer,
        in_specs=(
            P(TM_STREAM, None),
            P("stream", None),
            P("stream", None),
            P("stream", None),
            P("stream", None),
            P("stream", None),
            P(),
            P(),
            P(),
        ),
        out_specs=P(TM_STREAM, None),
        check_vma=False,
    )
```

```python
import jax
import jax.numpy as jnp
from jax import lax
from jax.experimental import pallas as pl
from jax.experimental.pallas import tpu as pltpu
from jax.sharding import Mesh
from jax.sharding import PartitionSpec as P

HEADS = 16
DK = 128
DV = 128
CHUNK = 128
GANG = 16
WIDE = 512
MAP_ROWS = 272
TM_STREAM = ("tm_0", "tm_1", "tm_2", "stream")
f32 = jnp.float32
bf16 = jnp.bfloat16


def mm(a, b, ca=1, cb=0):
    return lax.dot_general(
        a.astype(bf16), b.astype(bf16), (((ca,), (cb,)), ((), ())), preferred_element_type=f32
    )


def chunk_kernel(
    head_ref,
    rate_ref,
    bias_ref,
    token_ref,
    mine_ref,
    other_ref,
    reach_ref,
    own_ref,
    total_ref,
    raw_ref,
):
    step, steps = pl.program_id(0), pl.num_programs(0)
    rate, bias = rate_ref[head_ref[0]], bias_ref[head_ref[0]]
    size = token_ref.shape[0]
    rows = pl.ds(pl.multiple_of(step * size, size), size)
    half = mine_ref.shape[1]
    for c in range(2):
        weights = jnp.where(head_ref[1] == c, mine_ref[...], other_ref[...])
        raw_ref[rows, c * half : (c + 1) * half] = jnp.dot(
            token_ref[...], weights, preferred_element_type=f32
        )

    @pl.when(step == steps - 1)
    def _():
        delta_rule(rate, bias, raw_ref, reach_ref, own_ref, total_ref)


def delta_rule(rate, bias, raw_ref, reach_ref, own_ref, total_ref):
    row = lax.broadcasted_iota(jnp.int32, (CHUNK, CHUNK), 0)
    col = lax.broadcasted_iota(jnp.int32, (CHUNK, CHUNK), 1)
    strict, inclusive = row > col, row >= col
    eye = jnp.where(row == col, 1.0, 0.0).astype(f32)
    ones_below = jnp.where(inclusive, 1.0, 0.0).astype(bf16)

    def below(size):
        return (
            (row // (2 * size) == col // (2 * size))
            & ((row // size) % 2 == 1)
            & ((col // size) % 2 == 0)
        )

    state = jnp.concatenate([eye, jnp.zeros((DV, DK), f32)], 0)
    kept = jnp.ones((8, DK), f32)
    for first in range(0, raw_ref.shape[0] // CHUNK, GANG):
        starts = [(first + i) * CHUNK for i in range(GANG)]
        each = range(GANG)
        q, k, v, beta, grow, scale_row, beta_row, tail, last, decay = ([] for _ in range(10))
        for i in each:
            raw = raw_ref[pl.ds(starts[i], CHUNK), :]
            raw_q = raw[:, 0:128]
            raw_k = raw[:, 128:256]
            raw_v = raw[:, 256:384]
            logits = raw[:, 384:512]
            q.append(
                (
                    raw_q
                    * lax.rsqrt(jnp.sum(raw_q * raw_q, -1, keepdims=True) + 1e-06)
                    * DK ** (-0.5)
                ).astype(bf16)
            )
            k.append(
                (raw_k * lax.rsqrt(jnp.sum(raw_k * raw_k, -1, keepdims=True) + 1e-06)).astype(bf16)
            )
            v.append(raw_v.astype(bf16))
            x = logits[:, 0:1]
            softplus = jnp.maximum(x, 0.0) + jnp.log1p(jnp.exp(-jnp.abs(x)))
            log_decay = (-rate * softplus).astype(bf16)
            strength = (1.0 / (1.0 + jnp.exp(-(logits[:, 1:2] + bias)))).astype(bf16).astype(f32)
            g = mm(ones_below, jnp.broadcast_to(log_decay, (CHUNK, CHUNK)))
            b = jnp.broadcast_to(strength, (CHUNK, CHUNK))
            turned = jnp.where(col < 64, g, b).T
            g_row, b_row = turned[0:1, :], turned[64:65, :]
            g_last = g_row[:, CHUNK - 1 : CHUNK]
            beta.append(b)
            grow.append(jnp.exp(g))
            beta_row.append(b_row)
            scale_row.append(b_row * jnp.exp(g_row))
            tail.append(jnp.exp(g_last - g))
            last.append(jnp.exp(g_last))
            decay.append(jnp.exp(jnp.where(inclusive, g - g_row, 0.0)))
        both = [mm(jnp.concatenate([q[i], k[i]], 0), k[i], 1, 1) for i in each]
        scores = [jnp.where(inclusive, both[i][:CHUNK] * decay[i], 0.0) for i in each]
        lower = [jnp.where(strict, beta[i] * decay[i] * both[i][CHUNK:], 0.0) for i in each]
        inverse = [eye - jnp.where(below(1), lower[i], 0.0) for i in each]
        for size in (2, 4, 8, 16, 32, 64):
            mask = below(size)
            inner = [mm(jnp.where(mask, lower[i], 0.0), inverse[i]) for i in each]
            inverse = [inverse[i] - mm(inverse[i], inner[i]) for i in each]
        rounded = [inverse[i].astype(bf16) for i in each]
        high = [lower[i].astype(bf16) for i in each]
        rest = [eye - rounded[i].astype(f32) - mm(high[i], rounded[i]) for i in each]
        inverse = [rounded[i].astype(f32) + mm(rounded[i], rest[i]) for i in each]
        w = [mm(inverse[i] * scale_row[i], k[i]) for i in each]
        u = [mm(inverse[i] * beta_row[i], v[i]) for i in each]
        wu = [jnp.concatenate([w[i], u[i]], 1) for i in each]
        tail2 = [jnp.concatenate([tail[i], tail[i]], 1) for i in each]
        change = [mm(wu[i] * tail2[i], k[i], 0, 0) for i in each]
        inside = [mm(scores[i], wu[i]) for i in each]
        reach = [grow[i] * q[i].astype(f32) - inside[i][:, :DK] for i in each]
        for i in each:
            out = mm(reach[i], state, 1, 1)
            reach_ref[pl.ds(starts[i], CHUNK), :] = out[:, :DK].astype(bf16)
            own_ref[pl.ds(starts[i], CHUNK), :] = out[:, DK:] + inside[i][:, DK:]
            moved = mm(state, change[i][:DK])
            state = last[i] * state - moved
            state = jnp.concatenate([state[:DK], state[DK:] + change[i][DK:]], 0)
            kept = last[i] * kept
    part = kept.astype(bf16).astype(f32)
    total_ref[0:DK, :] = (state[:DK] - kept[0:1] * eye).astype(bf16)
    total_ref[DK : DK + DV, :] = state[DK:].astype(bf16)
    total_ref[DK + DV :, :] = jnp.concatenate([part, kept - part], 0).astype(bf16)


def opened(map_ref, *at):
    kept = map_ref[(*at, slice(DK + DV, MAP_ROWS))].astype(f32)
    change, shift = map_ref[(*at, slice(0, DK))], map_ref[(*at, slice(DK, DK + DV))]
    return change, shift.astype(f32), kept[0:1] + kept[8:9]


def after(state, change, shift, kept):
    return kept * state + mm(state, change) + shift


def join_kernel(place_ref, map_ref, before_ref, kept_ref, copies_ref):
    row = lax.broadcasted_iota(jnp.int32, (DK + DV, DK), 0)
    col = lax.broadcasted_iota(jnp.int32, (DK + DV, DK), 1)
    eye = jnp.where(row == col, 1.0, 0.0).astype(f32)
    state, decay = eye, jnp.ones((1, DK), f32)
    for j in range(map_ref.shape[0]):

        @pl.when(place_ref[1] == j)
        def _():
            before_ref[...] = state - decay * eye
            kept_ref[...] = jnp.broadcast_to(decay, (8, DK))

        change, shift, kept = opened(map_ref, j)
        state = after(state, change, jnp.concatenate([jnp.zeros((DK, DK), f32), shift], 0), kept)
        decay = kept * decay
    state = (state - decay * eye).astype(bf16)
    decay = jnp.broadcast_to(decay, (8, DK))
    part = decay.astype(bf16).astype(f32)
    decay = jnp.concatenate([part, decay - part], 0).astype(bf16)
    for i in range(copies_ref.shape[0]):
        copies_ref[i, 0 : DK + DV, :] = state
        copies_ref[i, DK + DV : MAP_ROWS, :] = decay


def read_kernel(place_ref, map_ref, before_ref, kept_ref, reach_ref, own_ref, read_ref):
    def one(j, state):
        return after(state, *opened(map_ref, j))

    state = lax.fori_loop(0, place_ref[0], one, jnp.zeros((DV, DK), f32))
    state = after(state, before_ref[0:DK, :], before_ref[DK:, :], kept_ref[0:1, :])
    read_ref[...] = (mm(reach_ref[...], state, 1, 1) + own_ref[...]).astype(bf16)


def shards(
    tokens, w_query, w_key, w_value, decay_proj, beta_proj, decay_rate, beta_bias, norm_gain
):
    local_rows = tokens.shape[0]
    streams = lax.axis_size("stream")
    head = lax.axis_index("stream")
    at_y, at_x, at_c = lax.axis_index("tm_0"), lax.axis_index("tm_1"), lax.axis_index("tm_2")
    vmem = pl.BlockSpec(memory_space=pltpu.VMEM)
    smem = pl.BlockSpec(memory_space=pltpu.SMEM)

    shares = 16
    rows = w_query.shape[0] // shares
    first = (at_y * 4 + at_x) * rows

    def share(w, width):
        return lax.dynamic_slice_in_dim(w, first, rows, 0).reshape(rows, HEADS, width)

    pads = jnp.zeros((rows, HEADS, WIDE - 386), bf16)
    left = jnp.concatenate([share(w_query, DK), share(w_key, DK)], -1)
    right = jnp.concatenate(
        [share(w_value, DV), share(decay_proj, 1), share(beta_proj, 1), pads], -1
    )
    weights = jnp.where(at_c == 0, left, right).transpose(1, 0, 2)
    all_tokens = lax.all_gather(tokens, "stream", axis=0, tiled=True)
    weights = lax.all_to_all(weights, "stream", split_axis=0, concat_axis=0, tiled=True)
    weights = jnp.broadcast_to(weights[None], (shares,) + weights.shape)
    weights = lax.all_to_all(weights, ("tm_0", "tm_1"), split_axis=0, concat_axis=0, tiled=True)
    weights = weights.transpose(1, 0, 2, 3).reshape(streams * shares * rows, WIDE // 2)
    swapped = lax.ppermute(weights, "tm_2", [(0, 1), (1, 0)])

    block_rows, features = all_tokens.shape
    steps = 2
    reach, own, total = pl.pallas_call(
        chunk_kernel,
        out_shape=(
            jax.ShapeDtypeStruct((block_rows, DK), bf16),
            jax.ShapeDtypeStruct((block_rows, DV), f32),
            jax.ShapeDtypeStruct((MAP_ROWS, DK), bf16),
        ),
        grid=(steps,),
        in_specs=[
            smem,
            smem,
            smem,
            pl.BlockSpec((block_rows // steps, features), lambda i: (i, 0)),
            pl.BlockSpec((features, WIDE // 2), lambda i: (0, 0)),
            pl.BlockSpec((features, WIDE // 2), lambda i: (0, 0)),
        ],
        out_specs=(
            pl.BlockSpec((block_rows, DK), lambda i: (0, 0)),
            pl.BlockSpec((block_rows, DV), lambda i: (0, 0)),
            pl.BlockSpec((MAP_ROWS, DK), lambda i: (0, 0)),
        ),
        scratch_shapes=[
            pltpu.VMEM((block_rows, WIDE), f32),
        ],
        compiler_params=pltpu.CompilerParams(vmem_limit_bytes=48 * 2**20),
    )(
        jnp.stack([head, at_c]).astype(jnp.int32),
        decay_rate,
        beta_bias,
        all_tokens,
        weights,
        swapped,
    )

    place = jnp.stack([at_y, at_x * 2 + at_c]).astype(jnp.int32)
    maps = lax.all_gather(total, ("tm_1", "tm_2"), axis=0)
    before, kept, maps = pl.pallas_call(
        join_kernel,
        out_shape=(
            jax.ShapeDtypeStruct((DK + DV, DK), f32),
            jax.ShapeDtypeStruct((8, DK), f32),
            jax.ShapeDtypeStruct((4, MAP_ROWS, DK), bf16),
        ),
        in_specs=[smem, vmem],
        out_specs=(vmem, vmem, vmem),
    )(place, maps)
    maps = lax.all_to_all(maps, "tm_0", split_axis=0, concat_axis=0, tiled=True)
    readout = pl.pallas_call(
        read_kernel,
        out_shape=jax.ShapeDtypeStruct((block_rows, DV), bf16),
        in_specs=[smem] + [vmem] * 5,
        out_specs=vmem,
        compiler_params=pltpu.CompilerParams(vmem_limit_bytes=32 * 2**20),
    )(place, maps, before, kept, reach, own)
    returned = lax.all_to_all(readout, "stream", split_axis=0, concat_axis=1, tiled=True)
    head_read = returned.reshape(local_rows, HEADS, DV).astype(f32)
    normed = (
        head_read
        * lax.rsqrt(jnp.mean(head_read * head_read, -1, keepdims=True) + 1e-06)
        * norm_gain
    )
    return normed.reshape(local_rows, HEADS * DV).astype(bf16)


def solution(mesh):
    finer = Mesh(
        mesh.devices.reshape(4, 4, 2, mesh.shape["stream"]), ("tm_0", "tm_1", "tm_2", "stream")
    )
    return jax.shard_map(
        shards,
        mesh=finer,
        in_specs=(
            P(TM_STREAM, None),
            P("stream", None),
            P("stream", None),
            P("stream", None),
            P("stream", None),
            P("stream", None),
            P(),
            P(),
            P(),
        ),
        out_specs=P(TM_STREAM, None),
        check_vma=False,
    )
```

```python
import jax
import jax.numpy as jnp
from jax import lax
from jax.experimental import pallas as pl
from jax.experimental.pallas import tpu as pltpu
from jax.sharding import Mesh
from jax.sharding import PartitionSpec as P

HEADS = 16
DK = 128
DV = 128
CHUNK = 128
GANG = 16
WIDE = 512
MAP_ROWS = 272
TM_STREAM = ("tm_0", "tm_1", "tm_2", "stream")
f32 = jnp.float32
bf16 = jnp.bfloat16


def mm(a, b, ca=1, cb=0):
    return lax.dot_general(
        a.astype(bf16), b.astype(bf16), (((ca,), (cb,)), ((), ())), preferred_element_type=f32
    )


def chunk_kernel(
    head_ref,
    rate_ref,
    bias_ref,
    token_ref,
    weight_ref,
    reach_ref,
    own_ref,
    total_ref,
    raw_ref,
):
    step, steps = pl.program_id(0), pl.num_programs(0)
    rate, bias = rate_ref[head_ref[0]], bias_ref[head_ref[0]]
    size = token_ref.shape[0]
    raw_ref[pl.ds(pl.multiple_of(step * size, size), size), :] = jnp.dot(
        token_ref[...], weight_ref[...], preferred_element_type=f32
    )

    @pl.when(step == steps - 1)
    def _():
        delta_rule(rate, bias, raw_ref, reach_ref, own_ref, total_ref)


def delta_rule(rate, bias, raw_ref, reach_ref, own_ref, total_ref):
    row = lax.broadcasted_iota(jnp.int32, (CHUNK, CHUNK), 0)
    col = lax.broadcasted_iota(jnp.int32, (CHUNK, CHUNK), 1)
    strict, inclusive = row > col, row >= col
    eye = jnp.where(row == col, 1.0, 0.0).astype(f32)
    ones_below = jnp.where(inclusive, 1.0, 0.0).astype(bf16)

    def below(size):
        return (
            (row // (2 * size) == col // (2 * size))
            & ((row // size) % 2 == 1)
            & ((col // size) % 2 == 0)
        )

    state = jnp.concatenate([eye, jnp.zeros((DV, DK), f32)], 0)
    kept = jnp.ones((8, DK), f32)
    for first in range(0, raw_ref.shape[0] // CHUNK, GANG):
        starts = [(first + i) * CHUNK for i in range(GANG)]
        each = range(GANG)
        q, k, v, beta, grow, scale_row, beta_row, tail, last, decay = ([] for _ in range(10))
        for i in each:
            raw = raw_ref[pl.ds(starts[i], CHUNK), :]
            raw_q = raw[:, 0:128]
            raw_k = raw[:, 128:256]
            raw_v = raw[:, 256:384]
            logits = raw[:, 384:512]
            q.append(
                (
                    raw_q
                    * lax.rsqrt(jnp.sum(raw_q * raw_q, -1, keepdims=True) + 1e-06)
                    * DK ** (-0.5)
                ).astype(bf16)
            )
            k.append(
                (raw_k * lax.rsqrt(jnp.sum(raw_k * raw_k, -1, keepdims=True) + 1e-06)).astype(bf16)
            )
            v.append(raw_v.astype(bf16))
            x = logits[:, 0:1]
            softplus = jnp.maximum(x, 0.0) + jnp.log1p(jnp.exp(-jnp.abs(x)))
            log_decay = (-rate * softplus).astype(bf16)
            strength = (1.0 / (1.0 + jnp.exp(-(logits[:, 1:2] + bias)))).astype(bf16).astype(f32)
            g = mm(ones_below, jnp.broadcast_to(log_decay, (CHUNK, CHUNK)))
            b = jnp.broadcast_to(strength, (CHUNK, CHUNK))
            turned = jnp.where(col < 64, g, b).T
            g_row, b_row = turned[0:1, :], turned[64:65, :]
            g_last = g_row[:, CHUNK - 1 : CHUNK]
            beta.append(b)
            grow.append(jnp.exp(g))
            beta_row.append(b_row)
            scale_row.append(b_row * jnp.exp(g_row))
            tail.append(jnp.exp(g_last - g))
            last.append(jnp.exp(g_last))
            decay.append(jnp.exp(jnp.where(inclusive, g - g_row, 0.0)))
        both = [mm(jnp.concatenate([q[i], k[i]], 0), k[i], 1, 1) for i in each]
        scores = [jnp.where(inclusive, both[i][:CHUNK] * decay[i], 0.0) for i in each]
        lower = [jnp.where(strict, beta[i] * decay[i] * both[i][CHUNK:], 0.0) for i in each]
        inverse = [eye - jnp.where(below(1), lower[i], 0.0) for i in each]
        for size in (2, 4, 8, 16, 32, 64):
            mask = below(size)
            inner = [mm(jnp.where(mask, lower[i], 0.0), inverse[i]) for i in each]
            inverse = [inverse[i] - mm(inverse[i], inner[i]) for i in each]
        rounded = [inverse[i].astype(bf16) for i in each]
        high = [lower[i].astype(bf16) for i in each]
        rest = [eye - rounded[i].astype(f32) - mm(high[i], rounded[i]) for i in each]
        inverse = [rounded[i].astype(f32) + mm(rounded[i], rest[i]) for i in each]
        w = [mm(inverse[i] * scale_row[i], k[i]) for i in each]
        u = [mm(inverse[i] * beta_row[i], v[i]) for i in each]
        wu = [jnp.concatenate([w[i], u[i]], 1) for i in each]
        tail2 = [jnp.concatenate([tail[i], tail[i]], 1) for i in each]
        change = [mm(wu[i] * tail2[i], k[i], 0, 0) for i in each]
        inside = [mm(scores[i], wu[i]) for i in each]
        reach = [grow[i] * q[i].astype(f32) - inside[i][:, :DK] for i in each]
        for i in each:
            out = mm(reach[i], state, 1, 1)
            reach_ref[pl.ds(starts[i], CHUNK), :] = out[:, :DK].astype(bf16)
            own_ref[pl.ds(starts[i], CHUNK), :] = out[:, DK:] + inside[i][:, DK:]
            moved = mm(state, change[i][:DK])
            state = last[i] * state - moved
            state = jnp.concatenate([state[:DK], state[DK:] + change[i][DK:]], 0)
            kept = last[i] * kept
    part = kept.astype(bf16).astype(f32)
    total_ref[0:DK, :] = (state[:DK] - kept[0:1] * eye).astype(bf16)
    total_ref[DK : DK + DV, :] = state[DK:].astype(bf16)
    total_ref[DK + DV :, :] = jnp.concatenate([part, kept - part], 0).astype(bf16)


def opened(map_ref, *at):
    kept = map_ref[(*at, slice(DK + DV, MAP_ROWS))].astype(f32)
    change, shift = map_ref[(*at, slice(0, DK))], map_ref[(*at, slice(DK, DK + DV))]
    return change, shift.astype(f32), kept[0:1] + kept[8:9]


def after(state, change, shift, kept):
    return kept * state + mm(state, change) + shift


def join_kernel(place_ref, map_ref, before_ref, kept_ref, copies_ref):
    row = lax.broadcasted_iota(jnp.int32, (DK + DV, DK), 0)
    col = lax.broadcasted_iota(jnp.int32, (DK + DV, DK), 1)
    eye = jnp.where(row == col, 1.0, 0.0).astype(f32)
    state, decay = eye, jnp.ones((1, DK), f32)
    for j in range(map_ref.shape[0]):

        @pl.when(place_ref[2] == j)
        def _():
            before_ref[...] = state - decay * eye
            kept_ref[...] = jnp.broadcast_to(decay, (8, DK))

        change, shift, kept = opened(map_ref, j)
        state = after(state, change, jnp.concatenate([jnp.zeros((DK, DK), f32), shift], 0), kept)
        decay = kept * decay
    state = (state - decay * eye).astype(bf16)
    decay = jnp.broadcast_to(decay, (8, DK))
    part = decay.astype(bf16).astype(f32)
    decay = jnp.concatenate([part, decay - part], 0).astype(bf16)
    for i in range(copies_ref.shape[0]):
        copies_ref[i, 0 : DK + DV, :] = state
        copies_ref[i, DK + DV : MAP_ROWS, :] = decay


def read_kernel(place_ref, map_ref, before_ref, kept_ref, reach_ref, own_ref, read_ref):
    def one(j, state):
        return after(state, *opened(map_ref, j))

    state = lax.fori_loop(0, place_ref[1], one, jnp.zeros((DV, DK), f32))
    state = after(state, before_ref[0:DK, :], before_ref[DK:, :], kept_ref[0:1, :])
    read_ref[...] = (mm(reach_ref[...], state, 1, 1) + own_ref[...]).astype(bf16)


def shards(
    tokens, w_query, w_key, w_value, decay_proj, beta_proj, decay_rate, beta_bias, norm_gain
):
    local_rows = tokens.shape[0]
    streams = lax.axis_size("stream")
    head = lax.axis_index("stream")
    at_y, at_x, at_c = lax.axis_index("tm_0"), lax.axis_index("tm_1"), lax.axis_index("tm_2")
    vmem = pl.BlockSpec(memory_space=pltpu.VMEM)
    smem = pl.BlockSpec(memory_space=pltpu.SMEM)

    shares = 16
    rows = w_query.shape[0] // shares
    first = (at_y * 4 + at_x) * rows

    def share(w, width):
        return lax.dynamic_slice_in_dim(w, first, rows, 0).reshape(rows, HEADS, width)

    pads = jnp.zeros((rows, HEADS, WIDE - 386), bf16)
    left = jnp.concatenate([share(w_query, DK), share(w_key, DK)], -1)
    right = jnp.concatenate(
        [share(w_value, DV), share(decay_proj, 1), share(beta_proj, 1), pads], -1
    )
    weights = jnp.where(at_c == 0, left, right).transpose(1, 0, 2)
    all_tokens = lax.all_gather(tokens, "stream", axis=0, tiled=True)
    weights = lax.all_to_all(weights, "stream", split_axis=0, concat_axis=0, tiled=True)
    weights = jnp.broadcast_to(weights[None], (shares,) + weights.shape)
    weights = lax.all_to_all(weights, ("tm_0", "tm_1"), split_axis=0, concat_axis=0, tiled=True)
    swapped = lax.ppermute(weights, "tm_2", [(0, 1), (1, 0)])
    halves = [
        jnp.where(at_c == 0, weights, swapped),
        jnp.where(at_c == 0, swapped, weights),
    ]
    weights = jnp.concatenate(halves, -1)
    weights = weights.transpose(1, 0, 2, 3).reshape(streams * shares * rows, WIDE)
    place = jnp.stack([head, at_y, at_x * 2 + at_c]).astype(jnp.int32)

    block_rows, features = all_tokens.shape
    steps = 2
    reach, own, total = pl.pallas_call(
        chunk_kernel,
        out_shape=(
            jax.ShapeDtypeStruct((block_rows, DK), bf16),
            jax.ShapeDtypeStruct((block_rows, DV), f32),
            jax.ShapeDtypeStruct((MAP_ROWS, DK), bf16),
        ),
        grid=(steps,),
        in_specs=[
            smem,
            smem,
            smem,
            pl.BlockSpec((block_rows // steps, features), lambda i: (i, 0)),
            pl.BlockSpec((features, WIDE), lambda i: (0, 0)),
        ],
        out_specs=(
            pl.BlockSpec((block_rows, DK), lambda i: (0, 0)),
            pl.BlockSpec((block_rows, DV), lambda i: (0, 0)),
            pl.BlockSpec((MAP_ROWS, DK), lambda i: (0, 0)),
        ),
        scratch_shapes=[
            pltpu.VMEM((block_rows, WIDE), f32),
        ],
        compiler_params=pltpu.CompilerParams(vmem_limit_bytes=48 * 2**20),
    )(
        place,
        decay_rate,
        beta_bias,
        all_tokens,
        weights,
    )

    maps = lax.all_gather(total, ("tm_1", "tm_2"), axis=0)
    before, kept, maps = pl.pallas_call(
        join_kernel,
        out_shape=(
            jax.ShapeDtypeStruct((DK + DV, DK), f32),
            jax.ShapeDtypeStruct((8, DK), f32),
            jax.ShapeDtypeStruct((4, MAP_ROWS, DK), bf16),
        ),
        in_specs=[smem, vmem],
        out_specs=(vmem, vmem, vmem),
    )(place, maps)
    maps = lax.all_to_all(maps, "tm_0", split_axis=0, concat_axis=0, tiled=True)
    readout = pl.pallas_call(
        read_kernel,
        out_shape=jax.ShapeDtypeStruct((block_rows, DV), bf16),
        in_specs=[smem] + [vmem] * 5,
        out_specs=vmem,
        compiler_params=pltpu.CompilerParams(vmem_limit_bytes=16 * 2**20),
    )(place, maps, before, kept, reach, own)
    returned = lax.all_to_all(readout, "stream", split_axis=0, concat_axis=1, tiled=True)
    head_read = returned.reshape(local_rows, HEADS, DV).astype(f32)
    normed = (
        head_read
        * lax.rsqrt(jnp.mean(head_read * head_read, -1, keepdims=True) + 1e-06)
        * norm_gain
    )
    return normed.reshape(local_rows, HEADS * DV).astype(bf16)


def solution(mesh):
    finer = Mesh(
        mesh.devices.reshape(4, 4, 2, mesh.shape["stream"]), ("tm_0", "tm_1", "tm_2", "stream")
    )
    return jax.shard_map(
        shards,
        mesh=finer,
        in_specs=(
            P(TM_STREAM, None),
            P("stream", None),
            P("stream", None),
            P("stream", None),
            P("stream", None),
            P("stream", None),
            P(),
            P(),
            P(),
        ),
        out_specs=P(TM_STREAM, None),
        check_vma=False,
    )
```

```python
import jax
import jax.numpy as jnp
from jax import lax
from jax.experimental import pallas as pl
from jax.experimental.pallas import tpu as pltpu
from jax.sharding import Mesh
from jax.sharding import PartitionSpec as P

HEADS = 16
DK = 128
DV = 128
CHUNK = 128
GANG = 16
WIDE = 512
MAP_ROWS = 272
TM_STREAM = ("tm_0", "tm_1", "tm_2", "stream")
f32 = jnp.float32
bf16 = jnp.bfloat16


def mm(a, b, ca=1, cb=0):
    return lax.dot_general(
        a.astype(bf16), b.astype(bf16), (((ca,), (cb,)), ((), ())), preferred_element_type=f32
    )


def chunk_kernel(
    head_ref,
    rate_ref,
    bias_ref,
    token_ref,
    weight_ref,
    reach_ref,
    own_ref,
    total_ref,
    raw_ref,
):
    step, steps = pl.program_id(0), pl.num_programs(0)
    rate, bias = rate_ref[head_ref[0]], bias_ref[head_ref[0]]
    size = token_ref.shape[0]
    raw_ref[pl.ds(pl.multiple_of(step * size, size), size), :] = jnp.dot(
        token_ref[...], weight_ref[...], preferred_element_type=f32
    )

    @pl.when(step == steps - 1)
    def _():
        delta_rule(rate, bias, raw_ref, reach_ref, own_ref, total_ref)


def delta_rule(rate, bias, raw_ref, reach_ref, own_ref, total_ref):
    row = lax.broadcasted_iota(jnp.int32, (CHUNK, CHUNK), 0)
    col = lax.broadcasted_iota(jnp.int32, (CHUNK, CHUNK), 1)
    strict, inclusive = row > col, row >= col
    eye = jnp.where(row == col, 1.0, 0.0).astype(f32)
    ones_below = jnp.where(inclusive, 1.0, 0.0).astype(bf16)

    def below(size):
        return (
            (row // (2 * size) == col // (2 * size))
            & ((row // size) % 2 == 1)
            & ((col // size) % 2 == 0)
        )

    state = jnp.concatenate([eye, jnp.zeros((DV, DK), f32)], 0)
    kept = jnp.ones((8, DK), f32)
    for first in range(0, raw_ref.shape[0] // CHUNK, GANG):
        starts = [(first + i) * CHUNK for i in range(GANG)]
        each = range(GANG)
        q, k, v, beta, grow, scale_row, beta_row, tail, last, decay = ([] for _ in range(10))
        for i in each:
            raw = raw_ref[pl.ds(starts[i], CHUNK), :]
            raw_q = raw[:, 0:128]
            raw_k = raw[:, 128:256]
            raw_v = raw[:, 256:384]
            logits = raw[:, 384:512]
            q.append(
                (
                    raw_q
                    * lax.rsqrt(jnp.sum(raw_q * raw_q, -1, keepdims=True) + 1e-06)
                    * DK ** (-0.5)
                ).astype(bf16)
            )
            k.append(
                (raw_k * lax.rsqrt(jnp.sum(raw_k * raw_k, -1, keepdims=True) + 1e-06)).astype(bf16)
            )
            v.append(raw_v.astype(bf16))
            x = logits[:, 0:1]
            softplus = jnp.maximum(x, 0.0) + jnp.log1p(jnp.exp(-jnp.abs(x)))
            log_decay = (-rate * softplus).astype(bf16)
            strength = (1.0 / (1.0 + jnp.exp(-(logits[:, 1:2] + bias)))).astype(bf16).astype(f32)
            g = mm(ones_below, jnp.broadcast_to(log_decay, (CHUNK, CHUNK)))
            b = jnp.broadcast_to(strength, (CHUNK, CHUNK))
            turned = jnp.where(col < 64, g, b).T
            g_row, b_row = turned[0:1, :], turned[64:65, :]
            g_last = g_row[:, CHUNK - 1 : CHUNK]
            beta.append(b)
            grow.append(jnp.exp(g))
            beta_row.append(b_row)
            scale_row.append(b_row * jnp.exp(g_row))
            tail.append(jnp.exp(g_last - g))
            last.append(jnp.exp(g_last))
            decay.append(jnp.exp(jnp.where(inclusive, g - g_row, 0.0)))
        both = [mm(jnp.concatenate([q[i], k[i]], 0), k[i], 1, 1) for i in each]
        scores = [jnp.where(inclusive, both[i][:CHUNK] * decay[i], 0.0) for i in each]
        lower = [jnp.where(strict, beta[i] * decay[i] * both[i][CHUNK:], 0.0) for i in each]
        inverse = [eye - jnp.where(below(1), lower[i], 0.0) for i in each]
        for size in (2, 4, 8, 16, 32, 64):
            mask = below(size)
            inner = [mm(jnp.where(mask, lower[i], 0.0), inverse[i]) for i in each]
            inverse = [inverse[i] - mm(inverse[i], inner[i]) for i in each]
        rounded = [inverse[i].astype(bf16) for i in each]
        high = [lower[i].astype(bf16) for i in each]
        rest = [eye - rounded[i].astype(f32) - mm(high[i], rounded[i]) for i in each]
        inverse = [rounded[i].astype(f32) + mm(rounded[i], rest[i]) for i in each]
        w = [mm(inverse[i] * scale_row[i], k[i]) for i in each]
        u = [mm(inverse[i] * beta_row[i], v[i]) for i in each]
        wu = [jnp.concatenate([w[i], u[i]], 1) for i in each]
        tail2 = [jnp.concatenate([tail[i], tail[i]], 1) for i in each]
        change = [mm(wu[i] * tail2[i], k[i], 0, 0) for i in each]
        inside = [mm(scores[i], wu[i]) for i in each]
        reach = [grow[i] * q[i].astype(f32) - inside[i][:, :DK] for i in each]
        for i in each:
            out = mm(reach[i], state, 1, 1)
            reach_ref[pl.ds(starts[i], CHUNK), :] = out[:, :DK].astype(bf16)
            own_ref[pl.ds(starts[i], CHUNK), :] = out[:, DK:] + inside[i][:, DK:]
            moved = mm(state, change[i][:DK])
            state = last[i] * state - moved
            state = jnp.concatenate([state[:DK], state[DK:] + change[i][DK:]], 0)
            kept = last[i] * kept
    part = kept.astype(bf16).astype(f32)
    total_ref[0:DK, :] = (state[:DK] - kept[0:1] * eye).astype(bf16)
    total_ref[DK : DK + DV, :] = state[DK:].astype(bf16)
    total_ref[DK + DV :, :] = jnp.concatenate([part, kept - part], 0).astype(bf16)


def opened(map_ref, *at):
    kept = map_ref[(*at, slice(DK + DV, MAP_ROWS))].astype(f32)
    change, shift = map_ref[(*at, slice(0, DK))], map_ref[(*at, slice(DK, DK + DV))]
    return change, shift.astype(f32), kept[0:1] + kept[8:9]


def join_kernel(place_ref, mine_ref, other_ref, copies_ref):
    def write(first_ref, second_ref):
        change, shift, kept = opened(first_ref)
        next_change, next_shift, next_kept = opened(second_ref)
        joined = kept * next_change.astype(f32) + next_kept * change.astype(f32)
        joined = (joined + mm(change, next_change)).astype(bf16)
        shift = (next_kept * shift + mm(shift, next_change) + next_shift).astype(bf16)
        kept = jnp.broadcast_to(kept * next_kept, (8, DK))
        part = kept.astype(bf16).astype(f32)
        kept = jnp.concatenate([part, kept - part], 0).astype(bf16)
        for i in range(copies_ref.shape[0]):
            copies_ref[i, 0:DK, :] = joined
            copies_ref[i, DK : DK + DV, :] = shift
            copies_ref[i, DK + DV : MAP_ROWS, :] = kept

    @pl.when(place_ref[2] == 0)
    def _():
        write(mine_ref, other_ref)

    @pl.when(place_ref[2] == 1)
    def _():
        write(other_ref, mine_ref)


def read_kernel(place_ref, map_ref, other_ref, reach_ref, own_ref, read_ref):
    def after(state, change, shift, kept):
        return kept * state + mm(state, change) + shift

    def one(j, state):
        return after(state, *opened(map_ref, j))

    state = lax.fori_loop(0, place_ref[1], one, jnp.zeros((DV, DK), f32))
    state = jnp.where(place_ref[2] == 1, after(state, *opened(other_ref)), state)
    read_ref[...] = (mm(reach_ref[...], state, 1, 1) + own_ref[...]).astype(bf16)


def shards(
    tokens, w_query, w_key, w_value, decay_proj, beta_proj, decay_rate, beta_bias, norm_gain
):
    local_rows = tokens.shape[0]
    streams = lax.axis_size("stream")
    head = lax.axis_index("stream")
    at_y, at_x, at_c = lax.axis_index("tm_0"), lax.axis_index("tm_1"), lax.axis_index("tm_2")
    vmem = pl.BlockSpec(memory_space=pltpu.VMEM)
    smem = pl.BlockSpec(memory_space=pltpu.SMEM)

    shares = 16
    rows = w_query.shape[0] // shares
    first = (at_y * 4 + at_x) * rows

    def share(w, width):
        return lax.dynamic_slice_in_dim(w, first, rows, 0).reshape(rows, HEADS, width)

    pads = jnp.zeros((rows, HEADS, WIDE - 386), bf16)
    left = jnp.concatenate([share(w_query, DK), share(w_key, DK)], -1)
    right = jnp.concatenate(
        [share(w_value, DV), share(decay_proj, 1), share(beta_proj, 1), pads], -1
    )
    weights = jnp.where(at_c == 0, left, right).transpose(1, 0, 2)
    all_tokens = lax.all_gather(tokens, "stream", axis=0, tiled=True)
    weights = lax.all_to_all(weights, "stream", split_axis=0, concat_axis=0, tiled=True)
    weights = jnp.broadcast_to(weights[None], (shares,) + weights.shape)
    weights = lax.all_to_all(weights, ("tm_0", "tm_1"), split_axis=0, concat_axis=0, tiled=True)
    swapped = lax.ppermute(weights, "tm_2", [(0, 1), (1, 0)])
    halves = [
        jnp.where(at_c == 0, weights, swapped),
        jnp.where(at_c == 0, swapped, weights),
    ]
    weights = jnp.concatenate(halves, -1)
    weights = weights.transpose(1, 0, 2, 3).reshape(streams * shares * rows, WIDE)
    place = jnp.stack([head, at_y * 4 + at_x, at_c]).astype(jnp.int32)

    block_rows, features = all_tokens.shape
    steps = 2
    reach, own, total = pl.pallas_call(
        chunk_kernel,
        out_shape=(
            jax.ShapeDtypeStruct((block_rows, DK), bf16),
            jax.ShapeDtypeStruct((block_rows, DV), f32),
            jax.ShapeDtypeStruct((MAP_ROWS, DK), bf16),
        ),
        grid=(steps,),
        in_specs=[
            smem,
            smem,
            smem,
            pl.BlockSpec((block_rows // steps, features), lambda i: (i, 0)),
            pl.BlockSpec((features, WIDE), lambda i: (0, 0)),
        ],
        out_specs=(
            pl.BlockSpec((block_rows, DK), lambda i: (0, 0)),
            pl.BlockSpec((block_rows, DV), lambda i: (0, 0)),
            pl.BlockSpec((MAP_ROWS, DK), lambda i: (0, 0)),
        ),
        scratch_shapes=[
            pltpu.VMEM((block_rows, WIDE), f32),
        ],
        compiler_params=pltpu.CompilerParams(vmem_limit_bytes=48 * 2**20),
    )(
        place,
        decay_rate,
        beta_bias,
        all_tokens,
        weights,
    )

    other = lax.ppermute(total, "tm_2", [(0, 1), (1, 0)])
    maps = pl.pallas_call(
        join_kernel,
        out_shape=jax.ShapeDtypeStruct((shares, MAP_ROWS, DK), bf16),
        in_specs=[smem, vmem, vmem],
        out_specs=vmem,
    )(place, total, other)
    maps = lax.all_to_all(maps, ("tm_0", "tm_1"), split_axis=0, concat_axis=0, tiled=True)
    readout = pl.pallas_call(
        read_kernel,
        out_shape=jax.ShapeDtypeStruct((block_rows, DV), bf16),
        in_specs=[smem, vmem, vmem, vmem, vmem],
        out_specs=vmem,
        compiler_params=pltpu.CompilerParams(vmem_limit_bytes=32 * 2**20),
    )(place, maps, other, reach, own)
    returned = lax.all_to_all(readout, "stream", split_axis=0, concat_axis=1, tiled=True)
    head_read = returned.reshape(local_rows, HEADS, DV).astype(f32)
    normed = (
        head_read
        * lax.rsqrt(jnp.mean(head_read * head_read, -1, keepdims=True) + 1e-06)
        * norm_gain
    )
    return normed.reshape(local_rows, HEADS * DV).astype(bf16)


def solution(mesh):
    finer = Mesh(
        mesh.devices.reshape(4, 4, 2, mesh.shape["stream"]), ("tm_0", "tm_1", "tm_2", "stream")
    )
    return jax.shard_map(
        shards,
        mesh=finer,
        in_specs=(
            P(TM_STREAM, None),
            P("stream", None),
            P("stream", None),
            P("stream", None),
            P("stream", None),
            P("stream", None),
            P(),
            P(),
            P(),
        ),
        out_specs=P(TM_STREAM, None),
        check_vma=False,
    )
```

```python
import jax
import jax.numpy as jnp
from jax import lax
from jax.experimental import pallas as pl
from jax.experimental.pallas import tpu as pltpu
from jax.sharding import Mesh
from jax.sharding import PartitionSpec as P

HEADS = 16
DK = 128
DV = 128
CHUNK = 128
GANG = 16
WIDE = 512
MAP_ROWS = 272
TM_STREAM = ("tm_0", "tm_1", "tm_2", "stream")
f32 = jnp.float32
bf16 = jnp.bfloat16


def mm(a, b, ca=1, cb=0):
    return lax.dot_general(
        a.astype(bf16), b.astype(bf16), (((ca,), (cb,)), ((), ())), preferred_element_type=f32
    )


def chunk_kernel(
    head_ref,
    rate_ref,
    bias_ref,
    token_ref,
    weight_ref,
    reach_ref,
    own_ref,
    total_ref,
    raw_ref,
):
    step, steps = pl.program_id(0), pl.num_programs(0)
    rate, bias = rate_ref[head_ref[0]], bias_ref[head_ref[0]]
    size = token_ref.shape[0]
    raw_ref[pl.ds(pl.multiple_of(step * size, size), size), :] = jnp.dot(
        token_ref[...], weight_ref[...], preferred_element_type=f32
    )

    @pl.when(step == steps - 1)
    def _():
        delta_rule(rate, bias, raw_ref, reach_ref, own_ref, total_ref)


def delta_rule(rate, bias, raw_ref, reach_ref, own_ref, total_ref):
    row = lax.broadcasted_iota(jnp.int32, (CHUNK, CHUNK), 0)
    col = lax.broadcasted_iota(jnp.int32, (CHUNK, CHUNK), 1)
    strict, inclusive = row > col, row >= col
    eye = jnp.where(row == col, 1.0, 0.0).astype(f32)
    ones_below = jnp.where(inclusive, 1.0, 0.0).astype(bf16)

    def below(size):
        return (
            (row // (2 * size) == col // (2 * size))
            & ((row // size) % 2 == 1)
            & ((col // size) % 2 == 0)
        )

    state = jnp.concatenate([eye, jnp.zeros((DV, DK), f32)], 0)
    kept = jnp.ones((8, DK), f32)
    for first in range(0, raw_ref.shape[0] // CHUNK, GANG):
        starts = [(first + i) * CHUNK for i in range(GANG)]
        each = range(GANG)
        q, k, v, beta, grow, scale_row, beta_row, tail, last, decay = ([] for _ in range(10))
        for i in each:
            raw = raw_ref[pl.ds(starts[i], CHUNK), :]
            raw_q = raw[:, 0:128]
            raw_k = raw[:, 128:256]
            raw_v = raw[:, 256:384]
            logits = raw[:, 384:512]
            q.append(
                (
                    raw_q
                    * lax.rsqrt(jnp.sum(raw_q * raw_q, -1, keepdims=True) + 1e-06)
                    * DK ** (-0.5)
                ).astype(bf16)
            )
            k.append(
                (raw_k * lax.rsqrt(jnp.sum(raw_k * raw_k, -1, keepdims=True) + 1e-06)).astype(bf16)
            )
            v.append(raw_v.astype(bf16))
            x = logits[:, 0:1]
            softplus = jnp.maximum(x, 0.0) + jnp.log1p(jnp.exp(-jnp.abs(x)))
            log_decay = (-rate * softplus).astype(bf16)
            strength = (1.0 / (1.0 + jnp.exp(-(logits[:, 1:2] + bias)))).astype(bf16).astype(f32)
            g = mm(ones_below, jnp.broadcast_to(log_decay, (CHUNK, CHUNK)))
            b = jnp.broadcast_to(strength, (CHUNK, CHUNK))
            turned = jnp.where(col < 64, g, b).T
            g_row, b_row = turned[0:1, :], turned[64:65, :]
            g_last = g_row[:, CHUNK - 1 : CHUNK]
            beta.append(b)
            grow.append(jnp.exp(g))
            beta_row.append(b_row)
            scale_row.append(b_row * jnp.exp(g_row))
            tail.append(jnp.exp(g_last - g))
            last.append(jnp.exp(g_last))
            decay.append(jnp.exp(jnp.where(inclusive, g - g_row, 0.0)))
        both = [mm(jnp.concatenate([q[i], k[i]], 0), k[i], 1, 1) for i in each]
        scores = [jnp.where(inclusive, both[i][:CHUNK] * decay[i], 0.0) for i in each]
        lower = [jnp.where(strict, beta[i] * decay[i] * both[i][CHUNK:], 0.0) for i in each]
        inverse = [eye - jnp.where(below(1), lower[i], 0.0) for i in each]
        for size in (2, 4, 8, 16, 32, 64):
            mask = below(size)
            inner = [mm(jnp.where(mask, lower[i], 0.0), inverse[i]) for i in each]
            inverse = [inverse[i] - mm(inverse[i], inner[i]) for i in each]
        rounded = [inverse[i].astype(bf16) for i in each]
        high = [lower[i].astype(bf16) for i in each]
        rest = [eye - rounded[i].astype(f32) - mm(high[i], rounded[i]) for i in each]
        inverse = [rounded[i].astype(f32) + mm(rounded[i], rest[i]) for i in each]
        w = [mm(inverse[i] * scale_row[i], k[i]) for i in each]
        u = [mm(inverse[i] * beta_row[i], v[i]) for i in each]
        wu = [jnp.concatenate([w[i], u[i]], 1) for i in each]
        tail2 = [jnp.concatenate([tail[i], tail[i]], 1) for i in each]
        change = [mm(wu[i] * tail2[i], k[i], 0, 0) for i in each]
        inside = [mm(scores[i], wu[i]) for i in each]
        reach = [grow[i] * q[i].astype(f32) - inside[i][:, :DK] for i in each]
        for i in each:
            out = mm(reach[i], state, 1, 1)
            reach_ref[pl.ds(starts[i], CHUNK), :] = out[:, :DK].astype(bf16)
            own_ref[pl.ds(starts[i], CHUNK), :] = out[:, DK:] + inside[i][:, DK:]
            moved = mm(state, change[i][:DK])
            state = last[i] * state - moved
            state = jnp.concatenate([state[:DK], state[DK:] + change[i][DK:]], 0)
            kept = last[i] * kept
    part = kept.astype(bf16).astype(f32)
    total_ref[0:DK, :] = (state[:DK] - kept[0:1] * eye).astype(bf16)
    total_ref[DK : DK + DV, :] = state[DK:].astype(bf16)
    total_ref[DK + DV :, :] = jnp.concatenate([part, kept - part], 0).astype(bf16)


def opened(map_ref, *at):
    kept = map_ref[(*at, slice(DK + DV, MAP_ROWS))].astype(f32)
    change, shift = map_ref[(*at, slice(0, DK))], map_ref[(*at, slice(DK, DK + DV))]
    return change, shift.astype(f32), kept[0:1] + kept[8:9]


def join_kernel(place_ref, mine_ref, other_ref, copies_ref):
    def write(first_ref, second_ref):
        change, shift, kept = opened(first_ref)
        next_change, next_shift, next_kept = opened(second_ref)
        joined = kept * next_change.astype(f32) + next_kept * change.astype(f32)
        joined = (joined + mm(change, next_change)).astype(bf16)
        shift = (next_kept * shift + mm(shift, next_change) + next_shift).astype(bf16)
        kept = jnp.broadcast_to(kept * next_kept, (8, DK))
        part = kept.astype(bf16).astype(f32)
        kept = jnp.concatenate([part, kept - part], 0).astype(bf16)
        for i in range(copies_ref.shape[0]):
            copies_ref[i, 0:DK, :] = joined
            copies_ref[i, DK : DK + DV, :] = shift
            copies_ref[i, DK + DV : MAP_ROWS, :] = kept

    @pl.when(place_ref[2] == 0)
    def _():
        write(mine_ref, other_ref)

    @pl.when(place_ref[2] == 1)
    def _():
        write(other_ref, mine_ref)


def read_kernel(place_ref, map_ref, other_ref, reach_ref, own_ref, read_ref):
    def after(state, change, shift, kept):
        return kept * state + mm(state, change) + shift

    def one(j, state):
        return after(state, *opened(map_ref, j))

    state = lax.fori_loop(0, place_ref[1], one, jnp.zeros((DV, DK), f32))
    state = jnp.where(place_ref[2] == 1, after(state, *opened(other_ref)), state)
    read_ref[...] = (mm(reach_ref[...], state, 1, 1) + own_ref[...]).astype(bf16)


def shards(
    tokens, w_query, w_key, w_value, decay_proj, beta_proj, decay_rate, beta_bias, norm_gain
):
    local_rows = tokens.shape[0]
    streams = lax.axis_size("stream")
    head = lax.axis_index("stream")
    at_y, at_x, at_c = lax.axis_index("tm_0"), lax.axis_index("tm_1"), lax.axis_index("tm_2")
    vmem = pl.BlockSpec(memory_space=pltpu.VMEM)
    smem = pl.BlockSpec(memory_space=pltpu.SMEM)

    shares = 16
    rows = w_query.shape[0] // shares
    first = (at_y * 4 + at_x) * rows

    def share(w, width):
        return lax.dynamic_slice_in_dim(w, first, rows, 0).reshape(rows, HEADS, width)

    pads = jnp.zeros((rows, HEADS, WIDE - 386), bf16)
    left = jnp.concatenate([share(w_query, DK), share(w_key, DK)], -1)
    right = jnp.concatenate(
        [share(w_value, DV), share(decay_proj, 1), share(beta_proj, 1), pads], -1
    )
    weights = jnp.where(at_c == 0, left, right).transpose(1, 0, 2)
    all_tokens = lax.all_gather(tokens, "stream", axis=0, tiled=True)
    weights = lax.all_to_all(weights, "stream", split_axis=0, concat_axis=0, tiled=True)
    weights = jnp.broadcast_to(weights[None], (shares,) + weights.shape)
    weights = lax.all_to_all(weights, ("tm_0", "tm_1"), split_axis=0, concat_axis=0, tiled=True)
    swapped = lax.ppermute(weights, "tm_2", [(0, 1), (1, 0)])
    halves = [
        jnp.where(at_c == 0, weights, swapped),
        jnp.where(at_c == 0, swapped, weights),
    ]
    weights = jnp.concatenate(halves, -1)
    weights = weights.transpose(1, 0, 2, 3).reshape(streams * shares * rows, WIDE)
    place = jnp.stack([head, at_y * 4 + at_x, at_c]).astype(jnp.int32)

    block_rows, features = all_tokens.shape
    steps = 4
    reach, own, total = pl.pallas_call(
        chunk_kernel,
        out_shape=(
            jax.ShapeDtypeStruct((block_rows, DK), bf16),
            jax.ShapeDtypeStruct((block_rows, DV), f32),
            jax.ShapeDtypeStruct((MAP_ROWS, DK), bf16),
        ),
        grid=(steps,),
        in_specs=[
            smem,
            smem,
            smem,
            pl.BlockSpec((block_rows // steps, features), lambda i: (i, 0)),
            pl.BlockSpec((features, WIDE), lambda i: (0, 0)),
        ],
        out_specs=(
            pl.BlockSpec((block_rows, DK), lambda i: (0, 0)),
            pl.BlockSpec((block_rows, DV), lambda i: (0, 0)),
            pl.BlockSpec((MAP_ROWS, DK), lambda i: (0, 0)),
        ),
        scratch_shapes=[
            pltpu.VMEM((block_rows, WIDE), f32),
        ],
        compiler_params=pltpu.CompilerParams(vmem_limit_bytes=48 * 2**20),
    )(
        place,
        decay_rate,
        beta_bias,
        all_tokens,
        weights,
    )

    other = lax.ppermute(total, "tm_2", [(0, 1), (1, 0)])
    maps = pl.pallas_call(
        join_kernel,
        out_shape=jax.ShapeDtypeStruct((shares, MAP_ROWS, DK), bf16),
        in_specs=[smem, vmem, vmem],
        out_specs=vmem,
    )(place, total, other)
    maps = lax.all_to_all(maps, ("tm_0", "tm_1"), split_axis=0, concat_axis=0, tiled=True)
    readout = pl.pallas_call(
        read_kernel,
        out_shape=jax.ShapeDtypeStruct((block_rows, DV), bf16),
        in_specs=[smem, vmem, vmem, vmem, vmem],
        out_specs=vmem,
        compiler_params=pltpu.CompilerParams(vmem_limit_bytes=32 * 2**20),
    )(place, maps, other, reach, own)
    returned = lax.all_to_all(readout, "stream", split_axis=0, concat_axis=1, tiled=True)
    head_read = returned.reshape(local_rows, HEADS, DV).astype(f32)
    normed = (
        head_read
        * lax.rsqrt(jnp.mean(head_read * head_read, -1, keepdims=True) + 1e-06)
        * norm_gain
    )
    return normed.reshape(local_rows, HEADS * DV).astype(bf16)


def solution(mesh):
    finer = Mesh(
        mesh.devices.reshape(4, 4, 2, mesh.shape["stream"]), ("tm_0", "tm_1", "tm_2", "stream")
    )
    return jax.shard_map(
        shards,
        mesh=finer,
        in_specs=(
            P(TM_STREAM, None),
            P("stream", None),
            P("stream", None),
            P("stream", None),
            P("stream", None),
            P("stream", None),
            P(),
            P(),
            P(),
        ),
        out_specs=P(TM_STREAM, None),
        check_vma=False,
    )
```
